32 devices in a mesh: group: 4 (over z), branch: 4 (over y, x), head: 2 (over core).
Axes of the slice: x: 2, y: 2, z: 4, core: 2. Of those that a mesh axis runs over, the one named last changes fastest.
Arguments:
- queries: bfloat16 [32, 64, 4096], P(('group', 'branch'), None, 'head'), may hold values from -6 to 6
- branch_keys: bfloat16 [32, 64, 512], P(('group', 'branch'), None, 'head'), may hold values from -6 to 6
- branch_values: bfloat16 [32, 64, 512], P(('group', 'branch'), None, 'head'), may hold values from -6 to 6
- prefix_keys: bfloat16 [64, 512], P('group', 'head'), may hold values from -6 to 6
- prefix_values: bfloat16 [64, 512], P('group', 'head'), may hold values from -6 to 6
- out_grad: bfloat16 [32, 64, 4096], P(('group', 'branch'), None, 'head'), may hold values from -6 to 6
- parents: int32 [32, 64], P(('group', 'branch')), may hold values from -1 to 62, as said below
- lengths: int32 [32], P(('group', 'branch')), may hold values from 16 to 64
Outputs:
- query_grad: bfloat16 [32, 64, 4096], P(('group', 'branch'), None, 'head')
- branch_key_grad: bfloat16 [32, 64, 512], P(('group', 'branch'), None, 'head')
- branch_value_grad: bfloat16 [32, 64, 512], P(('group', 'branch'), None, 'head')
- prefix_key_grad: bfloat16 [64, 512], P('group', 'head')
- prefix_value_grad: bfloat16 [64, 512], P('group', 'head')
The draws below stay inside these ranges and needn't reach their ends.
Inputs may be any that keep to these rules, and one draw needn't show every extreme that they name: parents[b, t] is -1 or an earlier slot of the same branch, within four slots of t.
All inputs are finite; a program needn't handle non-finite values.
Results may differ from the reference program's by a relative error of at most 0.012.
Values may be sent and summed in bfloat16 or wider, within the bound.
No kernel may reach another device: no remote copies, remote signals or barrier semaphores. Data moves between devices by JAX's collectives and lax.ppermute only.
A program may use at most 64 MiB of HBM per device.

```python
import jax
import jax.numpy as jnp
from jax import lax

QH = 32
KVH = 4
HD = 128
BLEN = 64
BRANCHES = 32
PREFIX = 64


def draw_queries(key, part):
    key = jax.random.fold_in(key, 1)
    drawn = jax.random.normal(key, (BRANCHES, BLEN, QH * HD), jnp.float32)
    drawn = jnp.clip(drawn, -6.0, 6.0)
    return drawn.astype(jnp.bfloat16)


def draw_prefix_keys(key, part):
    key = jax.random.fold_in(key, 2)
    drawn = jnp.clip(jax.random.normal(key, (PREFIX, KVH * HD), jnp.float32), -6.0, 6.0)
    return drawn.astype(jnp.bfloat16)


def draw_parents(key, part):
    key = jax.random.fold_in(key, 3)
    steps_back = jax.random.randint(key, (BRANCHES, BLEN), 1, 5, jnp.int32)
    slots = jnp.arange(BLEN, dtype=jnp.int32)[None, :]
    steps_back = jnp.where(slots == BLEN - 1, 1, steps_back)
    return jnp.maximum(slots - steps_back, -1).astype(jnp.int32)


def draw_lengths(key, part):
    key = jax.random.fold_in(key, 4)
    drawn = jax.random.randint(key, (BRANCHES,), BLEN // 4, BLEN + 1, jnp.int32)
    indices = jnp.arange(BRANCHES, dtype=jnp.int32)
    drawn = jnp.where(indices == 0, BLEN, drawn)
    drawn = jnp.where(indices == 1, BLEN // 4, drawn)
    return drawn.astype(jnp.int32)


def block_levels(own_key, extent, split, smallest, high):
    def one(dim, shards_of):
        draws = jax.random.uniform(jax.random.fold_in(jax.random.fold_in(own_key, 6), dim), (shards_of,), jnp.float32, smallest / len(split), high / len(split))
        return jnp.repeat(jnp.exp(draws), extent[dim] // shards_of).reshape((-1,) + (1,) * (len(extent) - dim - 1))

    gain = one(*split[0])
    for cut in split[1:]:
        gain = gain * one(*cut)
    return gain


def gaussian(stream_key, extent, spread, limit, pieces=(), kind=jnp.bfloat16):
    entries = spread * jax.random.normal(stream_key, extent, jnp.float32)
    if pieces:
        entries = entries * block_levels(stream_key, extent, pieces, -0.22, 0.18)
    return jnp.clip(entries, -limit, limit).astype(kind)


def setup_inputs(seed: int = 0) -> dict:
    key_list = jax.random.split(jax.random.key(seed), 9)
    queries = draw_queries(jax.random.fold_in(key_list[8], 71), 0)
    branch_keys = gaussian(key_list[1], (BRANCHES, BLEN, KVH * HD), 1.0, 6.0, ((0, 16), (2, 2)))
    branch_values = gaussian(key_list[2], (BRANCHES, BLEN, KVH * HD), 1.0, 6.0, ((0, 16), (2, 2)))
    prefix_keys = draw_prefix_keys(jax.random.fold_in(key_list[8], 71), 0)
    prefix_values = gaussian(key_list[4], (PREFIX, KVH * HD), 1.0, 6.0, ((0, 4), (1, 2)))
    out_grad = gaussian(key_list[5], (BRANCHES, BLEN, QH * HD), 1.0, 6.0, ((0, 16), (2, 2)))
    parents = draw_parents(jax.random.fold_in(key_list[8], 71), 0)
    lengths = draw_lengths(jax.random.fold_in(key_list[8], 71), 0)
    return dict(queries=queries, branch_keys=branch_keys, branch_values=branch_values, prefix_keys=prefix_keys, prefix_values=prefix_values, out_grad=out_grad, parents=parents, lengths=lengths)


def ancestors(parents):
    length = parents.shape[-1]
    positions = jnp.arange(length, dtype=jnp.int32)
    reach = jnp.broadcast_to(positions[:, None] == positions[None, :], parents.shape + (length,))
    pointer = parents
    for rounds in range((length - 1).bit_length()):
        linked = pointer >= 0
        target = jnp.where(linked, pointer, 0).astype(jnp.int32)
        lifted = jnp.take_along_axis(reach, jnp.broadcast_to(target[..., None], reach.shape), axis=1)
        reach = reach | (lifted & linked[..., None])
        pointer = jnp.where(linked, jnp.take_along_axis(pointer, target, axis=1), -1).astype(jnp.int32)
    return reach


def reference(queries, branch_keys, branch_values, prefix_keys, prefix_values, out_grad, parents, lengths):
    factor = HD ** -0.5
    per_group = QH // KVH
    count, length = parents.shape
    reach = ancestors(parents)
    positions = jnp.arange(length, dtype=jnp.int32)
    live = (positions[None, :] < lengths[:, None]).astype(jnp.float32)
    live_rows = live.reshape(-1, 1)

    def kv_head(head_index):
        start = (head_index * HD).astype(jnp.int32)
        pre_keys = lax.dynamic_slice_in_dim(prefix_keys, start, HD, 1)
        pre_values = lax.dynamic_slice_in_dim(prefix_values, start, HD, 1)
        tree_keys = lax.dynamic_slice_in_dim(branch_keys, start, HD, 2).astype(jnp.float32)
        tree_values = lax.dynamic_slice_in_dim(branch_values, start, HD, 2).astype(jnp.float32)

        def one_head(carry, member):
            column = ((head_index * per_group + member) * HD).astype(jnp.int32)
            head_query = lax.dynamic_slice_in_dim(queries, column, HD, 2)
            head_grad = lax.dynamic_slice_in_dim(out_grad, column, HD, 2)
            query_rows = head_query.reshape(-1, HD)
            grad_rows = head_grad.reshape(-1, HD)
            query_float = head_query.astype(jnp.float32)
            grad_float = head_grad.astype(jnp.float32)
            pre_scores = factor * jnp.dot(query_rows, pre_keys.T, preferred_element_type=jnp.float32)
            tree_scores = factor * jnp.einsum("blh,buh->blu", query_float, tree_keys)
            tree_scores = jnp.where(reach, tree_scores, -jnp.inf)
            row_max = jnp.maximum(jnp.max(pre_scores, axis=1).reshape(count, length), jnp.max(tree_scores, axis=2))
            totals = jnp.sum(jnp.exp(pre_scores - row_max.reshape(-1, 1)), axis=1).reshape(count, length)
            totals = totals + jnp.sum(jnp.exp(tree_scores - row_max[..., None]), axis=2)
            log_total = row_max + jnp.log(totals)
            pre_weights = jnp.exp(pre_scores - log_total.reshape(-1, 1)) * live_rows
            tree_weights = jnp.exp(tree_scores - log_total[..., None]) * live[..., None]
            pre_rounded = pre_weights.astype(jnp.bfloat16)
            tree_rounded = tree_weights.astype(jnp.bfloat16)
            attended = jnp.dot(pre_rounded, pre_values, preferred_element_type=jnp.float32).reshape(count, length, HD)
            attended = attended + jnp.einsum("blu,buh->blh", tree_rounded.astype(jnp.float32), tree_values)
            delta = jnp.sum(grad_float * attended, axis=2)
            pre_dweights = jnp.dot(grad_rows, pre_values.T, preferred_element_type=jnp.float32)
            tree_dweights = jnp.einsum("blh,buh->blu", grad_float, tree_values)
            pre_dscores = (pre_weights * (pre_dweights - delta.reshape(-1, 1))).astype(jnp.bfloat16)
            tree_dscores = (tree_weights * (tree_dweights - delta[..., None])).astype(jnp.bfloat16)
            tree_dfloat = tree_dscores.astype(jnp.float32)
            query_grad = jnp.dot(pre_dscores, pre_keys, preferred_element_type=jnp.float32).reshape(count, length, HD)
            query_grad = factor * (query_grad + jnp.einsum("blu,buh->blh", tree_dfloat, tree_keys))
            key_sum, value_sum, tree_key_sum, tree_value_sum = carry
            key_sum = key_sum + factor * jnp.dot(pre_dscores.T, query_rows, preferred_element_type=jnp.float32)
            value_sum = value_sum + jnp.dot(pre_rounded.T, grad_rows, preferred_element_type=jnp.float32)
            tree_key_sum = tree_key_sum + factor * jnp.einsum("blu,blh->buh", tree_dfloat, query_float)
            tree_value_sum = tree_value_sum + jnp.einsum("blu,blh->buh", tree_rounded.astype(jnp.float32), grad_float)
            return (key_sum, value_sum, tree_key_sum, tree_value_sum), query_grad.astype(jnp.bfloat16)

        prefix_zero = jnp.zeros((prefix_keys.shape[0], HD), jnp.float32)
        tree_zero = jnp.zeros((count, length, HD), jnp.float32)
        sums, grads = lax.scan(one_head, (prefix_zero, prefix_zero, tree_zero, tree_zero), jnp.arange(per_group, dtype=jnp.int32))
        return grads, sums[0], sums[1], sums[2], sums[3]

    grads, key_sums, value_sums, tree_key_sums, tree_value_sums = lax.map(kv_head, jnp.arange(KVH, dtype=jnp.int32))
    query_grad = jnp.transpose(grads, (2, 3, 0, 1, 4)).reshape(count, length, QH * HD)
    branch_key_grad = jnp.transpose(tree_key_sums, (1, 2, 0, 3)).reshape(count, length, KVH * HD).astype(jnp.bfloat16)
    branch_value_grad = jnp.transpose(tree_value_sums, (1, 2, 0, 3)).reshape(count, length, KVH * HD).astype(jnp.bfloat16)
    prefix_key_grad = jnp.transpose(key_sums, (1, 0, 2)).reshape(-1, KVH * HD).astype(jnp.bfloat16)
    prefix_value_grad = jnp.transpose(value_sums, (1, 0, 2)).reshape(-1, KVH * HD).astype(jnp.bfloat16)
    return (query_grad, branch_key_grad, branch_value_grad, prefix_key_grad, prefix_value_grad)
```

```python
import functools

import jax
import jax.numpy as jnp
from jax import lax
from jax.experimental import pallas as pl
from jax.experimental.pallas import tpu as pltpu
from jax.sharding import PartitionSpec as P

QH = 32
KVH = 4
HD = 128
PER = QH // KVH
RADIX = 4
LOG2E = 1.4426950408889634
NT = (((1,), (1,)), ((), ()))
NN = (((1,), (0,)), ((), ()))
TN = (((0,), (0,)), ((), ()))


def dot(a, b, dims):
    return lax.dot_general(a, b, dims, preferred_element_type=jnp.float32)


def digits(size):
    out, stride = [], 1
    while stride < size:
        count = min(RADIX, size // stride)
        while (size // stride) % count:
            count -= 1
        if count == 1:
            count = size // stride
        out.append((stride, count))
        stride *= count
    return out


def moved(size, stride, count, step, sign):
    pairs = []
    for i in range(size):
        digit = (i // stride) % count
        if count & (count - 1) == 0:
            other = digit ^ step
        else:
            other = (digit + sign * step) % count
        pairs.append((i, i + (other - digit) * stride))
    return pairs


def gather_parts(x, axis, size):
    parts = [x]
    for stride, count in digits(size):
        block = parts[0] if len(parts) == 1 else jnp.stack(parts)
        out = list(parts)
        for step in range(1, count):
            got = lax.ppermute(block, axis, moved(size, stride, count, step, 1))
            out += [got] if len(parts) == 1 else [got[i] for i in range(len(parts))]
        parts = out
    return parts


def scatter_sum(parts, axis, size):
    for stride, count in reversed(digits(size)):
        low = len(parts) // count
        total = parts[0] if low == 1 else jnp.stack(parts[:low])
        terms = [total]
        for step in range(1, count):
            piece = parts[step * low : (step + 1) * low]
            block = piece[0] if low == 1 else jnp.stack(piece)
            terms.append(lax.ppermute(block, axis, moved(size, stride, count, step, -1)))
        total = functools.reduce(jnp.add, terms)
        parts = [total] if low == 1 else [total[i] for i in range(low)]
    return parts[0]


def all_sum(x, axis, size):
    for stride, count in digits(size):
        terms = [x]
        for step in range(1, count):
            terms.append(lax.ppermute(x, axis, moved(size, stride, count, step, 1)))
        x = functools.reduce(jnp.add, terms)
    return x


def kernel(*refs, parts):
    q_ref, g_ref, bk_ref, bv_ref, par_ref, len_ref = refs[:6]
    pre_refs = refs[6 : 6 + parts]
    dq_ref, dbk_ref, dbv_ref = refs[6 + parts : 9 + parts]
    out_refs = refs[9 + parts :]
    count, length, _ = q_ref.shape
    rows = pre_refs[0].shape[0]
    prefix = rows * parts
    heads = bk_ref.shape[2] // HD
    factor = HD**-0.5
    pre = jnp.concatenate([r[...] for r in pre_refs], axis=0)
    width = heads * HD

    slot = lax.broadcasted_iota(jnp.int32, (length, length), 0)
    token = lax.broadcasted_iota(jnp.int32, (length, length), 1)
    masks = []
    for b in range(count):
        hit = (slot == token) | (slot == par_ref[b : b + 1, :])
        reach = hit.astype(jnp.float32).astype(jnp.bfloat16)
        for rounds in range((length - 1).bit_length()):
            paths = dot(reach, reach, NN)
            reach = jnp.minimum(paths, 1.0).astype(jnp.bfloat16)
        wide = jnp.concatenate([reach.astype(jnp.float32)] * PER, axis=1)
        masks.append(wide > 0.5)
    place = lax.broadcasted_iota(jnp.int32, (1, PER * length), 1) % length

    for h in range(heads):
        low = h * HD
        key_sum = value_sum = None
        for b in range(count):
            keys = jnp.concatenate([pre[:, low : low + HD], bk_ref[b, :, low : low + HD]], axis=0)
            values = jnp.concatenate(
                [pre[:, width + low : width + low + HD], bv_ref[b, :, low : low + HD]], axis=0
            )
            cols = [slice((h * PER + m) * HD, (h * PER + m + 1) * HD) for m in range(PER)]
            q = jnp.concatenate([q_ref[b, :, c] for c in cols], axis=0)
            g = jnp.concatenate([g_ref[b, :, c] for c in cols], axis=0)
            live = (place < len_ref[b]).astype(jnp.float32)
            scores = dot(keys, q, NT) * (factor * LOG2E)
            scores = jnp.concatenate(
                [scores[:prefix], jnp.where(masks[b], scores[prefix:], -1e30)], axis=0
            )
            dweights = dot(values, g, NT)
            powers = jnp.exp2(scores - jnp.max(scores, axis=0, keepdims=True))
            weights = powers * (live / jnp.sum(powers, axis=0, keepdims=True))
            rounded = weights.astype(jnp.bfloat16)
            delta = jnp.sum(rounded.astype(jnp.float32) * dweights, axis=0, keepdims=True)
            dscores = (weights * (dweights - delta)).astype(jnp.bfloat16)
            value_grad = dot(rounded, g, NN)
            key_grad = dot(dscores, q, NN) * factor
            query_grad = (dot(dscores, keys, TN) * factor).astype(jnp.bfloat16)
            for m, c in enumerate(cols):
                dq_ref[b, :, c] = query_grad[m * length : (m + 1) * length]
            dbk_ref[b, :, low : low + HD] = key_grad[prefix:].astype(jnp.bfloat16)
            dbv_ref[b, :, low : low + HD] = value_grad[prefix:].astype(jnp.bfloat16)
            key_sum = key_grad[:prefix] if b == 0 else key_sum + key_grad[:prefix]
            value_sum = value_grad[:prefix] if b == 0 else value_sum + value_grad[:prefix]
        for i, ref in enumerate(out_refs):
            ref[:, low : low + HD] = key_sum[i * rows : (i + 1) * rows]
            ref[:, width + low : width + low + HD] = value_sum[i * rows : (i + 1) * rows]


def body(
    queries, branch_keys, branch_values, prefix_keys, prefix_values, out_grad, parents, lengths,
    *, groups, branches
):
    packed = jnp.concatenate([prefix_keys, prefix_values], axis=1)
    parts = gather_parts(packed, "group", groups)
    vmem = pl.BlockSpec(memory_space=pltpu.VMEM)
    outs = pl.pallas_call(
        functools.partial(kernel, parts=groups),
        out_shape=[
            jax.ShapeDtypeStruct(queries.shape, jnp.bfloat16),
            jax.ShapeDtypeStruct(branch_keys.shape, jnp.bfloat16),
            jax.ShapeDtypeStruct(branch_values.shape, jnp.bfloat16),
        ]
        + [jax.ShapeDtypeStruct(packed.shape, jnp.float32)] * groups,
        in_specs=[vmem] * 5 + [pl.BlockSpec(memory_space=pltpu.SMEM)] + [vmem] * groups,
        out_specs=[vmem] * (3 + groups),
        compiler_params=pltpu.CompilerParams(vmem_limit_bytes=48 * 1024 * 1024),
    )(queries, out_grad, branch_keys, branch_values, parents, lengths, *parts)
    owned = scatter_sum(outs[3:], "group", groups)
    total = all_sum(owned, "branch", branches).astype(jnp.bfloat16)
    half = prefix_keys.shape[1]
    return outs[0], outs[1], outs[2], total[:, :half], total[:, half:]


def solution(mesh):
    sharded = P(("group", "branch"), None, "head")
    return jax.shard_map(
        functools.partial(body, groups=mesh.shape["group"], branches=mesh.shape["branch"]),
        mesh=mesh,
        in_specs=(
            sharded,
            sharded,
            sharded,
            P("group", "head"),
            P("group", "head"),
            sharded,
            P(("group", "branch"), None),
            P(("group", "branch")),
        ),
        out_specs=(sharded, sharded, sharded, P("group", "head"), P("group", "head")),
        check_vma=False,
    )
```

```python
import functools

import jax
import jax.numpy as jnp
from jax import lax
from jax.experimental import pallas as pl
from jax.experimental.pallas import tpu as pltpu
from jax.sharding import PartitionSpec as P

QH = 32
KVH = 4
HD = 128
PER = QH // KVH
RADIX = 4
LOG2E = 1.4426950408889634
NT = (((1,), (1,)), ((), ()))
NN = (((1,), (0,)), ((), ()))
TN = (((0,), (0,)), ((), ()))


def dot(a, b, dims):
    return lax.dot_general(a, b, dims, preferred_element_type=jnp.float32)


def digits(size):
    out, stride = [], 1
    while stride < size:
        count = min(RADIX, size // stride)
        while (size // stride) % count:
            count -= 1
        if count == 1:
            count = size // stride
        out.append((stride, count))
        stride *= count
    return out


def moved(size, stride, count, step, sign):
    pairs = []
    for i in range(size):
        digit = (i // stride) % count
        if count & (count - 1) == 0:
            other = digit ^ step
        else:
            other = (digit + sign * step) % count
        pairs.append((i, i + (other - digit) * stride))
    return pairs


def gather_parts(x, axis, size):
    parts = [x]
    for stride, count in digits(size):
        block = parts[0] if len(parts) == 1 else jnp.stack(parts)
        out = list(parts)
        for step in range(1, count):
            got = lax.ppermute(block, axis, moved(size, stride, count, step, 1))
            out += [got] if len(parts) == 1 else [got[i] for i in range(len(parts))]
        parts = out
    return parts


def tree_sum(terms):
    while len(terms) > 1:
        terms = [a + b for a, b in zip(terms[::2], terms[1::2])] + terms[len(terms) & ~1 :]
    return terms[0]


def scatter_sum(parts, axis, size):
    for stride, count in reversed(digits(size)):
        low = len(parts) // count
        terms = [parts[0].astype(jnp.float32) if low == 1 else jnp.stack(parts[:low]).astype(jnp.float32)]
        for step in range(1, count):
            piece = parts[step * low : (step + 1) * low]
            block = piece[0] if low == 1 else jnp.stack(piece)
            got = lax.ppermute(block, axis, moved(size, stride, count, step, -1))
            terms.append(got.astype(jnp.float32))
        total = tree_sum(terms).astype(parts[0].dtype)
        parts = [total] if low == 1 else [total[i] for i in range(low)]
    return parts[0]


def all_sum(x, axis, size):
    for stride, count in digits(size):
        terms = [x]
        for step in range(1, count):
            terms.append(lax.ppermute(x, axis, moved(size, stride, count, step, 1)))
        x = tree_sum([t.astype(jnp.float32) for t in terms]).astype(x.dtype)
    return x


def head_rows(ref, b, h):
    cols = [slice((h * PER + m) * HD, (h * PER + m + 1) * HD) for m in range(PER)]
    return jnp.concatenate([ref[b, :, c] for c in cols], axis=0)


def tree_kernel(
    q_hbm, g_hbm, bk_hbm, bv_hbm, par_ref, len_ref,
    q_ref, g_ref, bk_ref, power_ref, dweight_ref, max_ref, sum_ref, dot_ref, live_ref,
    bv_ref, sems,
):
    count, length, _ = q_ref.shape
    heads = bk_ref.shape[2] // HD
    pairs = ((q_hbm, q_ref), (g_hbm, g_ref), (bk_hbm, bk_ref), (bv_hbm, bv_ref))
    copies = [pltpu.make_async_copy(s, d, sems.at[i]) for i, (s, d) in enumerate(pairs)]
    for copy in copies:
        copy.start()
    slot = lax.broadcasted_iota(jnp.int32, (length, length), 0)
    token = lax.broadcasted_iota(jnp.int32, (length, length), 1)
    reaches = []
    for b in range(count):
        hit = (slot == token) | (slot == par_ref[b : b + 1, :])
        reaches.append(hit.astype(jnp.float32).astype(jnp.bfloat16))
    for rounds in range((length - 1).bit_length()):
        reaches = [jnp.minimum(dot(r, r, NN), 1.0).astype(jnp.bfloat16) for r in reaches]
    masks = [jnp.concatenate([r.astype(jnp.float32)] * PER, axis=1) > 0.5 for r in reaches]
    place = lax.broadcasted_iota(jnp.int32, (1, PER * length), 1) % length
    lives = [(place < len_ref[b]).astype(jnp.float32) for b in range(count)]
    for copy in copies:
        copy.wait()
    for h in range(heads):
        low = h * HD
        for b in range(count):
            i = h * count + b
            scores = dot(bk_ref[b, :, low : low + HD], head_rows(q_ref, b, h), NT)
            dweights = dot(bv_ref[b, :, low : low + HD], head_rows(g_ref, b, h), NT)
            scores = jnp.where(masks[b], scores * (HD**-0.5 * LOG2E), -1e30)
            top = jnp.max(scores, axis=0, keepdims=True)
            powers = jnp.exp2(scores - top)
            power_ref[i] = powers
            dweight_ref[i] = dweights
            live_ref[i] = lives[b]
            max_ref[i] = top
            sum_ref[i] = jnp.sum(powers, axis=0, keepdims=True)
            dot_ref[i] = jnp.sum(powers * dweights, axis=0, keepdims=True)


def prefix_kernel(*refs, parts):
    q_ref, g_ref, max_ref, sum_ref, dot_ref, live_ref = refs[:6]
    pre_refs = refs[6 : 6 + parts]
    dscore_ref, scale_ref, delta_ref = refs[6 + parts : 9 + parts]
    out_refs = refs[9 + parts :]
    count, length, _ = q_ref.shape
    rows, width = pre_refs[0].shape
    width //= 2
    heads = width // HD
    factor = HD**-0.5
    pre = jnp.concatenate([r[...] for r in pre_refs], axis=0)
    for h in range(heads):
        low = h * HD
        keys = pre[:, low : low + HD]
        values = pre[:, width + low : width + low + HD]
        key_sum = value_sum = None
        for b in range(count):
            i = h * count + b
            q = head_rows(q_ref, b, h)
            g = head_rows(g_ref, b, h)
            scores = dot(keys, q, NT) * (factor * LOG2E)
            dweights = dot(values, g, NT)
            tree_max = max_ref[i]
            top = jnp.maximum(jnp.max(scores, axis=0, keepdims=True), tree_max)
            powers = jnp.exp2(scores - top)
            tree = jnp.exp2(tree_max - top)
            scale = live_ref[i] / (jnp.sum(powers, axis=0, keepdims=True) + tree * sum_ref[i])
            delta = scale * (
                jnp.sum(powers * dweights, axis=0, keepdims=True) + tree * dot_ref[i]
            )
            weights = powers * scale
            dscores = (weights * (dweights - delta)).astype(jnp.bfloat16)
            value_grad = dot(weights.astype(jnp.bfloat16), g, NN)
            key_grad = dot(dscores, q, NN) * factor
            dscore_ref[i] = dscores
            scale_ref[i] = scale * tree
            delta_ref[i] = delta
            key_sum = key_grad if b == 0 else key_sum + key_grad
            value_sum = value_grad if b == 0 else value_sum + value_grad
        for i, ref in enumerate(out_refs):
            ref[:, low : low + HD] = key_sum[i * rows : (i + 1) * rows].astype(ref.dtype)
            ref[:, width + low : width + low + HD] = value_sum[i * rows : (i + 1) * rows].astype(
                ref.dtype
            )


def branch_kernel(*refs, parts):
    q_ref, g_ref, bk_ref, power_ref, dweight_ref, dscore_ref, scale_ref, delta_ref = refs[:8]
    pre_refs = refs[8 : 8 + parts]
    dq_ref, dbk_ref, dbv_ref = refs[8 + parts :]
    count, length, _ = q_ref.shape
    heads = bk_ref.shape[2] // HD
    factor = HD**-0.5
    pre = jnp.concatenate([r[:, : heads * HD] for r in pre_refs], axis=0)
    for h in range(heads):
        low = h * HD
        for b in range(count):
            i = h * count + b
            weights = power_ref[i] * scale_ref[i]
            dscores = (weights * (dweight_ref[i] - delta_ref[i])).astype(jnp.bfloat16)
            tree_keys = bk_ref[b, :, low : low + HD]
            value_grad = dot(weights.astype(jnp.bfloat16), head_rows(g_ref, b, h), NN)
            key_grad = dot(dscores, head_rows(q_ref, b, h), NN) * factor
            dbk_ref[b, :, low : low + HD] = key_grad.astype(jnp.bfloat16)
            dbv_ref[b, :, low : low + HD] = value_grad.astype(jnp.bfloat16)
            both = jnp.concatenate([dscore_ref[i], dscores], axis=0)
            keys = jnp.concatenate([pre[:, low : low + HD], tree_keys], axis=0)
            query_grad = (dot(both, keys, TN) * factor).astype(jnp.bfloat16)
            for m in range(PER):
                col = (h * PER + m) * HD
                dq_ref[b, :, col : col + HD] = query_grad[m * length : (m + 1) * length]


def body(
    queries, branch_keys, branch_values, prefix_keys, prefix_values, out_grad, parents, lengths,
    *, groups, branches
):
    count, length, columns = queries.shape
    heads = branch_keys.shape[2] // HD
    prefix = prefix_keys.shape[0] * groups
    packed = jnp.concatenate([prefix_keys, prefix_values], axis=1)
    parts = gather_parts(packed, "group", groups)
    vmem = pl.BlockSpec(memory_space=pltpu.VMEM)
    smem = pl.BlockSpec(memory_space=pltpu.SMEM)
    anywhere = pl.BlockSpec(memory_space=pltpu.HBM)
    hbm = lambda x: pltpu.with_memory_space_constraint(x, pltpu.HBM)
    params = pltpu.CompilerParams(vmem_limit_bytes=16 * 1024 * 1024)
    wide = PER * length
    row = jax.ShapeDtypeStruct((heads * count, 1, wide), jnp.float32)
    block = jax.ShapeDtypeStruct((heads * count, length, wide), jnp.float32)
    like = lambda x: jax.ShapeDtypeStruct(x.shape, x.dtype)
    work = heads * count * wide * HD * 2
    q, g, keys, powers, dweights, tops, sums, dots, live = pl.pallas_call(
        tree_kernel,
        out_shape=[like(queries), like(out_grad), like(branch_keys), block, block, row, row, row, row],
        in_specs=[anywhere] * 4 + [vmem, smem],
        out_specs=[vmem] * 9,
        scratch_shapes=[
            pltpu.VMEM(branch_values.shape, branch_values.dtype),
            pltpu.SemaphoreType.DMA((4,)),
        ],
        compiler_params=params,
        cost_estimate=pl.CostEstimate(
            flops=2 * work * length, bytes_accessed=2 * queries.size * 2, transcendentals=wide * length * 4
        ),
        name="tree",
    )(*(hbm(x) for x in (queries, out_grad, branch_keys, branch_values)), parents, lengths)
    outs = pl.pallas_call(
        functools.partial(prefix_kernel, parts=groups),
        out_shape=[
            jax.ShapeDtypeStruct((heads * count, prefix, wide), jnp.bfloat16), row, row
        ]
        + [like(packed)] * groups,
        in_specs=[vmem] * (6 + groups),
        out_specs=[vmem] * (3 + groups),
        compiler_params=params,
        cost_estimate=pl.CostEstimate(
            flops=4 * work * prefix, bytes_accessed=0, transcendentals=wide * prefix * 4
        ),
        name="prefix",
    )(q, g, tops, sums, dots, live, *parts)
    query_grad, branch_key_grad, branch_value_grad = pl.pallas_call(
        functools.partial(branch_kernel, parts=groups),
        out_shape=[like(queries), like(branch_keys), like(branch_values)],
        in_specs=[vmem] * (8 + groups),
        out_specs=[vmem] * 3,
        compiler_params=params,
        cost_estimate=pl.CostEstimate(
            flops=4 * work * length, bytes_accessed=queries.size * 2, transcendentals=0
        ),
        name="branch",
    )(q, g, keys, powers, dweights, *outs[:3], *parts)
    owned = scatter_sum(outs[3:], "group", groups)
    total = all_sum(owned, "branch", branches)
    half = prefix_keys.shape[1]
    return query_grad, branch_key_grad, branch_value_grad, total[:, :half], total[:, half:]


def solution(mesh):
    sharded = P(("group", "branch"), None, "head")
    return jax.shard_map(
        functools.partial(body, groups=mesh.shape["group"], branches=mesh.shape["branch"]),
        mesh=mesh,
        in_specs=(
            sharded,
            sharded,
            sharded,
            P("group", "head"),
            P("group", "head"),
            sharded,
            P(("group", "branch"), None),
            P(("group", "branch")),
        ),
        out_specs=(sharded, sharded, sharded, P("group", "head"), P("group", "head")),
        check_vma=False,
    )
```

```python
import functools

import jax
import jax.numpy as jnp
from jax import lax
from jax.experimental import pallas as pl
from jax.experimental.pallas import tpu as pltpu
from jax.sharding import PartitionSpec as P

QH = 32
KVH = 4
HD = 128
PER = QH // KVH
RADIX = 4
GATHER = (2, 3, 1)
SCATTER = (3, 2, 1)
SUM = (3, 2, 1)
LOG2E = 1.4426950408889634
NT = (((1,), (1,)), ((), ()))
NN = (((1,), (0,)), ((), ()))
TN = (((0,), (0,)), ((), ()))


def dot(a, b, dims):
    return lax.dot_general(a, b, dims, preferred_element_type=jnp.float32)


def digits(size):
    out, stride = [], 1
    while stride < size:
        count = min(RADIX, size // stride)
        while (size // stride) % count:
            count -= 1
        if count == 1:
            count = size // stride
        out.append((stride, count))
        stride *= count
    return out


def moved(size, stride, count, step, sign):
    pairs = []
    for i in range(size):
        digit = (i // stride) % count
        if count & (count - 1) == 0:
            other = digit ^ step
        else:
            other = (digit + sign * step) % count
        pairs.append((i, i + (other - digit) * stride))
    return pairs


def in_order(count, order):
    return [step for step in order if step < count] + list(range(len(order) + 1, count))


def exchange(blocks, axis, size, stride, steps, sign):
    count = len(steps) + 1
    return [
        lax.ppermute(block, axis, moved(size, stride, count, step, sign))
        for block, step in zip(blocks, steps)
    ]


def gather_parts(x, axis, size):
    parts = [x]
    for stride, count in digits(size):
        low = len(parts)
        block = x if low == 1 else jnp.stack(parts)
        steps = in_order(count, GATHER)
        for got in exchange([block] * (count - 1), axis, size, stride, steps, 1):
            parts += [got] if low == 1 else [got[i] for i in range(low)]
    return parts


def tree_sum(terms):
    while len(terms) > 1:
        terms = [a + b for a, b in zip(terms[::2], terms[1::2])] + terms[len(terms) & ~1 :]
    return terms[0]


def scatter_sum(parts, axis, size):
    parts, dtype = list(parts), parts[0].dtype
    for stride, count in reversed(digits(size)):
        low = len(parts) // count
        blocks = parts if low == 1 else [
            jnp.stack(parts[i * low : (i + 1) * low]) for i in range(count)
        ]
        found = dict(zip(in_order(count, GATHER), blocks[1:]))
        steps = in_order(count, SCATTER)
        terms = blocks[:1] + exchange([found[s] for s in steps], axis, size, stride, steps, -1)
        total = tree_sum([t.astype(jnp.float32) for t in terms]).astype(dtype)
        parts = [total] if low == 1 else [total[i] for i in range(low)]
    return parts[0]


def all_sum(x, axis, size):
    for stride, count in digits(size):
        steps = in_order(count, SUM)
        terms = [x] + exchange([x] * (count - 1), axis, size, stride, steps, 1)
        x = tree_sum([t.astype(jnp.float32) for t in terms]).astype(x.dtype)
    return x


def head_rows(ref, b, h):
    cols = [slice((h * PER + m) * HD, (h * PER + m + 1) * HD) for m in range(PER)]
    return jnp.concatenate([ref[b, :, c] for c in cols], axis=0)


def tree_kernel(
    q_hbm, g_hbm, bk_hbm, bv_hbm, par_ref, len_ref,
    q_ref, g_ref, bk_ref, power_ref, dweight_ref, max_ref, sum_ref, dot_ref, live_ref,
    bv_ref, sems,
):
    count, length, _ = q_ref.shape
    heads = bk_ref.shape[2] // HD
    pairs = ((q_hbm, q_ref), (g_hbm, g_ref), (bk_hbm, bk_ref), (bv_hbm, bv_ref))
    copies = [pltpu.make_async_copy(s, d, sems.at[i]) for i, (s, d) in enumerate(pairs)]
    for copy in copies:
        copy.start()
    slot = lax.broadcasted_iota(jnp.int32, (length, length), 0)
    token = lax.broadcasted_iota(jnp.int32, (length, length), 1)
    reaches = []
    for b in range(count):
        hit = (slot == token) | (slot == par_ref[b : b + 1, :])
        reaches.append(hit.astype(jnp.float32).astype(jnp.bfloat16))
    for rounds in range((length - 1).bit_length()):
        reaches = [jnp.minimum(dot(r, r, NN), 1.0).astype(jnp.bfloat16) for r in reaches]
    masks = [jnp.concatenate([r.astype(jnp.float32)] * PER, axis=1) > 0.5 for r in reaches]
    place = lax.broadcasted_iota(jnp.int32, (1, PER * length), 1) % length
    lives = [(place < len_ref[b]).astype(jnp.float32) for b in range(count)]
    for copy in copies:
        copy.wait()
    for h in range(heads):
        low = h * HD
        for b in range(count):
            i = h * count + b
            scores = dot(bk_ref[b, :, low : low + HD], head_rows(q_ref, b, h), NT)
            dweights = dot(bv_ref[b, :, low : low + HD], head_rows(g_ref, b, h), NT)
            scores = jnp.where(masks[b], scores * (HD**-0.5 * LOG2E), -1e30)
            top = jnp.max(scores, axis=0, keepdims=True)
            powers = jnp.exp2(scores - top)
            power_ref[i] = powers
            dweight_ref[i] = dweights
            live_ref[i] = lives[b]
            max_ref[i] = top
            sum_ref[i] = jnp.sum(powers, axis=0, keepdims=True)
            dot_ref[i] = jnp.sum(powers * dweights, axis=0, keepdims=True)


def prefix_kernel(*refs, parts):
    q_ref, g_ref, max_ref, sum_ref, dot_ref, live_ref = refs[:6]
    pre_refs = refs[6 : 6 + parts]
    dscore_ref, scale_ref, delta_ref = refs[6 + parts : 9 + parts]
    out_refs = refs[9 + parts :]
    count, length, _ = q_ref.shape
    rows, width = pre_refs[0].shape
    width //= 2
    heads = width // HD
    factor = HD**-0.5
    pre = jnp.concatenate([r[...] for r in pre_refs], axis=0)
    for h in range(heads):
        low = h * HD
        keys = pre[:, low : low + HD]
        values = pre[:, width + low : width + low + HD]
        key_sum = value_sum = None
        for b in range(count):
            i = h * count + b
            q = head_rows(q_ref, b, h)
            g = head_rows(g_ref, b, h)
            scores = dot(keys, q, NT) * (factor * LOG2E)
            dweights = dot(values, g, NT)
            tree_max = max_ref[i]
            top = jnp.maximum(jnp.max(scores, axis=0, keepdims=True), tree_max)
            powers = jnp.exp2(scores - top)
            tree = jnp.exp2(tree_max - top)
            scale = live_ref[i] / (jnp.sum(powers, axis=0, keepdims=True) + tree * sum_ref[i])
            delta = scale * (
                jnp.sum(powers * dweights, axis=0, keepdims=True) + tree * dot_ref[i]
            )
            weights = powers * scale
            dscores = (weights * (dweights - delta)).astype(jnp.bfloat16)
            value_grad = dot(weights.astype(jnp.bfloat16), g, NN)
            key_grad = dot(dscores, q, NN) * factor
            dscore_ref[i] = dscores
            scale_ref[i] = scale * tree
            delta_ref[i] = delta
            key_sum = key_grad if b == 0 else key_sum + key_grad
            value_sum = value_grad if b == 0 else value_sum + value_grad
        for i, ref in enumerate(out_refs):
            ref[:, low : low + HD] = key_sum[i * rows : (i + 1) * rows].astype(ref.dtype)
            ref[:, width + low : width + low + HD] = value_sum[i * rows : (i + 1) * rows].astype(
                ref.dtype
            )


def branch_kernel(*refs, parts):
    q_ref, g_ref, bk_ref, power_ref, dweight_ref, dscore_ref, scale_ref, delta_ref = refs[:8]
    pre_refs = refs[8 : 8 + parts]
    dq_ref, dbk_ref, dbv_ref = refs[8 + parts :]
    count, length, _ = q_ref.shape
    heads = bk_ref.shape[2] // HD
    factor = HD**-0.5
    pre = jnp.concatenate([r[:, : heads * HD] for r in pre_refs], axis=0)
    for h in range(heads):
        low = h * HD
        for b in range(count):
            i = h * count + b
            weights = power_ref[i] * scale_ref[i]
            dscores = (weights * (dweight_ref[i] - delta_ref[i])).astype(jnp.bfloat16)
            tree_keys = bk_ref[b, :, low : low + HD]
            value_grad = dot(weights.astype(jnp.bfloat16), head_rows(g_ref, b, h), NN)
            key_grad = dot(dscores, head_rows(q_ref, b, h), NN) * factor
            dbk_ref[b, :, low : low + HD] = key_grad.astype(jnp.bfloat16)
            dbv_ref[b, :, low : low + HD] = value_grad.astype(jnp.bfloat16)
            both = jnp.concatenate([dscore_ref[i], dscores], axis=0)
            keys = jnp.concatenate([pre[:, low : low + HD], tree_keys], axis=0)
            query_grad = (dot(both, keys, TN) * factor).astype(jnp.bfloat16)
            for m in range(PER):
                col = (h * PER + m) * HD
                dq_ref[b, :, col : col + HD] = query_grad[m * length : (m + 1) * length]


def body(
    queries, branch_keys, branch_values, prefix_keys, prefix_values, out_grad, parents, lengths,
    *, groups, branches
):
    count, length, columns = queries.shape
    heads = branch_keys.shape[2] // HD
    prefix = prefix_keys.shape[0] * groups
    packed = jnp.concatenate([prefix_keys, prefix_values], axis=1)
    parts = gather_parts(packed, "group", groups)
    vmem = pl.BlockSpec(memory_space=pltpu.VMEM)
    smem = pl.BlockSpec(memory_space=pltpu.SMEM)
    anywhere = pl.BlockSpec(memory_space=pltpu.HBM)
    hbm = lambda x: pltpu.with_memory_space_constraint(x, pltpu.HBM)
    params = pltpu.CompilerParams(vmem_limit_bytes=16 * 1024 * 1024)
    wide = PER * length
    row = jax.ShapeDtypeStruct((heads * count, 1, wide), jnp.float32)
    block = jax.ShapeDtypeStruct((heads * count, length, wide), jnp.float32)
    like = lambda x: jax.ShapeDtypeStruct(x.shape, x.dtype)
    work = heads * count * wide * HD * 2
    q, g, keys, powers, dweights, tops, sums, dots, live = pl.pallas_call(
        tree_kernel,
        out_shape=[like(queries), like(out_grad), like(branch_keys), block, block, row, row, row, row],
        in_specs=[anywhere] * 4 + [vmem, smem],
        out_specs=[vmem] * 9,
        scratch_shapes=[
            pltpu.VMEM(branch_values.shape, branch_values.dtype),
            pltpu.SemaphoreType.DMA((4,)),
        ],
        compiler_params=params,
        cost_estimate=pl.CostEstimate(
            flops=2 * work * length, bytes_accessed=2 * queries.size * 2, transcendentals=wide * length * 4
        ),
        name="tree",
    )(*(hbm(x) for x in (queries, out_grad, branch_keys, branch_values)), parents, lengths)
    outs = pl.pallas_call(
        functools.partial(prefix_kernel, parts=groups),
        out_shape=[
            jax.ShapeDtypeStruct((heads * count, prefix, wide), jnp.bfloat16), row, row
        ]
        + [like(packed)] * groups,
        in_specs=[vmem] * (6 + groups),
        out_specs=[vmem] * (3 + groups),
        compiler_params=params,
        cost_estimate=pl.CostEstimate(
            flops=4 * work * prefix, bytes_accessed=0, transcendentals=wide * prefix * 4
        ),
        name="prefix",
    )(q, g, tops, sums, dots, live, *parts)
    query_grad, branch_key_grad, branch_value_grad = pl.pallas_call(
        functools.partial(branch_kernel, parts=groups),
        out_shape=[like(queries), like(branch_keys), like(branch_values)],
        in_specs=[vmem] * (8 + groups),
        out_specs=[vmem] * 3,
        compiler_params=params,
        cost_estimate=pl.CostEstimate(
            flops=4 * work * length, bytes_accessed=queries.size * 2, transcendentals=0
        ),
        name="branch",
    )(q, g, keys, powers, dweights, *outs[:3], *parts)
    owned = scatter_sum(outs[3:], "group", groups)
    total = all_sum(owned, "branch", branches)
    half = prefix_keys.shape[1]
    return query_grad, branch_key_grad, branch_value_grad, total[:, :half], total[:, half:]


def solution(mesh):
    sharded = P(("group", "branch"), None, "head")
    return jax.shard_map(
        functools.partial(body, groups=mesh.shape["group"], branches=mesh.shape["branch"]),
        mesh=mesh,
        in_specs=(
            sharded,
            sharded,
            sharded,
            P("group", "head"),
            P("group", "head"),
            sharded,
            P(("group", "branch"), None),
            P(("group", "branch")),
        ),
        out_specs=(sharded, sharded, sharded, P("group", "head"), P("group", "head")),
        check_vma=False,
    )
```

```python
import functools

import jax
import jax.numpy as jnp
from jax import lax
from jax.experimental import pallas as pl
from jax.experimental.pallas import tpu as pltpu
from jax.sharding import PartitionSpec as P

QH = 32
KVH = 4
HD = 128
PER = QH // KVH
RADIX = 4
GATHER = (3, 2, 1)
SCATTER = (3, 2, 1)
SUM = (3, 2, 1)
LOG2E = 1.4426950408889634
NT = (((1,), (1,)), ((), ()))
NN = (((1,), (0,)), ((), ()))
TN = (((0,), (0,)), ((), ()))


def dot(a, b, dims):
    return lax.dot_general(a, b, dims, preferred_element_type=jnp.float32)


def digits(size):
    out, stride = [], 1
    while stride < size:
        count = min(RADIX, size // stride)
        while (size // stride) % count:
            count -= 1
        if count == 1:
            count = size // stride
        out.append((stride, count))
        stride *= count
    return out


def moved(size, stride, count, step, sign):
    pairs = []
    for i in range(size):
        digit = (i // stride) % count
        if count & (count - 1) == 0:
            other = digit ^ step
        else:
            other = (digit + sign * step) % count
        pairs.append((i, i + (other - digit) * stride))
    return pairs


def in_order(count, order):
    return [step for step in order if step < count] + list(range(len(order) + 1, count))


def exchange(blocks, axis, size, stride, steps, sign):
    count = len(steps) + 1
    return [
        lax.ppermute(block, axis, moved(size, stride, count, step, sign))
        for block, step in zip(blocks, steps)
    ]


def gather_parts(x, axis, size):
    parts = [x]
    for stride, count in digits(size):
        low = len(parts)
        block = x if low == 1 else jnp.stack(parts)
        steps = in_order(count, GATHER)
        for got in exchange([block] * (count - 1), axis, size, stride, steps, 1):
            parts += [got] if low == 1 else [got[i] for i in range(low)]
    return parts


def tree_sum(terms):
    while len(terms) > 1:
        terms = [a + b for a, b in zip(terms[::2], terms[1::2])] + terms[len(terms) & ~1 :]
    return terms[0]


def scatter_sum(parts, axis, size):
    parts, dtype = list(parts), parts[0].dtype
    for stride, count in reversed(digits(size)):
        low = len(parts) // count
        blocks = parts if low == 1 else [
            jnp.stack(parts[i * low : (i + 1) * low]) for i in range(count)
        ]
        found = dict(zip(in_order(count, GATHER), blocks[1:]))
        steps = in_order(count, SCATTER)
        terms = blocks[:1] + exchange([found[s] for s in steps], axis, size, stride, steps, -1)
        total = tree_sum([t.astype(jnp.float32) for t in terms]).astype(dtype)
        parts = [total] if low == 1 else [total[i] for i in range(low)]
    return parts[0]


def all_sum(x, axis, size):
    for stride, count in digits(size):
        steps = in_order(count, SUM)
        terms = [x] + exchange([x] * (count - 1), axis, size, stride, steps, 1)
        x = tree_sum([t.astype(jnp.float32) for t in terms]).astype(x.dtype)
    return x


def head_rows(ref, b, h):
    cols = [slice((h * PER + m) * HD, (h * PER + m + 1) * HD) for m in range(PER)]
    return jnp.concatenate([ref[b, :, c] for c in cols], axis=0)


def tree_kernel(
    q_hbm, g_hbm, bk_hbm, bv_hbm, par_ref, len_ref,
    q_ref, g_ref, bk_ref, power_ref, dweight_ref, max_ref, sum_ref, dot_ref, live_ref,
    bv_ref, sems,
):
    count, length, _ = q_ref.shape
    heads = bk_ref.shape[2] // HD
    pairs = [(q_hbm.at[0], q_ref.at[0]), (g_hbm.at[0], g_ref.at[0])]
    pairs += [(bk_hbm, bk_ref), (bv_hbm, bv_ref)]
    for b in range(1, count):
        pairs += [(q_hbm.at[b], q_ref.at[b]), (g_hbm.at[b], g_ref.at[b])]
    copies = [pltpu.make_async_copy(s, d, sems.at[i]) for i, (s, d) in enumerate(pairs)]
    for copy in copies:
        copy.start()
    slot = lax.broadcasted_iota(jnp.int32, (length, length), 0)
    token = lax.broadcasted_iota(jnp.int32, (length, length), 1)
    reaches = []
    for b in range(count):
        hit = (slot == token) | (slot == par_ref[b : b + 1, :])
        reaches.append(hit.astype(jnp.float32).astype(jnp.bfloat16))
    for rounds in range((length - 1).bit_length()):
        reaches = [jnp.minimum(dot(r, r, NN), 1.0).astype(jnp.bfloat16) for r in reaches]
    masks = [jnp.concatenate([r.astype(jnp.float32)] * PER, axis=1) > 0.5 for r in reaches]
    place = lax.broadcasted_iota(jnp.int32, (1, PER * length), 1) % length
    for b in range(count):
        for copy in copies[2 * b + 2 if b else 0 : 2 * b + 4]:
            copy.wait()
        stage = []
        for h in range(heads):
            cols = slice(h * HD, (h + 1) * HD)
            stage.append((
                dot(bk_ref[b, :, cols], head_rows(q_ref, b, h), NT),
                dot(bv_ref[b, :, cols], head_rows(g_ref, b, h), NT),
            ))
        live = (place < len_ref[:, b : b + 1]).astype(jnp.float32)
        for h, (scores, dweights) in enumerate(stage):
            i = h * count + b
            scores = jnp.where(masks[b], scores * (HD**-0.5 * LOG2E), -1e30)
            top = jnp.max(scores, axis=0, keepdims=True)
            powers = jnp.exp2(scores - top)
            power_ref[i] = powers
            dweight_ref[i] = dweights
            live_ref[i] = live
            max_ref[i] = top
            sum_ref[i] = jnp.sum(powers, axis=0, keepdims=True)
            dot_ref[i] = jnp.sum(powers * dweights, axis=0, keepdims=True)


def prefix_kernel(*refs, parts):
    q_ref, g_ref, max_ref, sum_ref, dot_ref, live_ref = refs[:6]
    pre_refs = refs[6 : 6 + parts]
    dscore_ref, scale_ref, delta_ref = refs[6 + parts : 9 + parts]
    out_refs = refs[9 + parts :]
    count, length, _ = q_ref.shape
    rows, width = pre_refs[0].shape
    width //= 2
    heads = width // HD
    factor = HD**-0.5
    pre = jnp.concatenate([r[...] for r in pre_refs], axis=0)
    stage = []
    for h in range(heads):
        low = h * HD
        keys = pre[:, low : low + HD]
        values = pre[:, width + low : width + low + HD]
        for b in range(count):
            q = head_rows(q_ref, b, h)
            g = head_rows(g_ref, b, h)
            stage.append((q, g, dot(keys, q, NT), dot(values, g, NT)))
    ready = []
    for i, (q, g, scores, dweights) in enumerate(stage):
        scores = scores * (factor * LOG2E)
        tree_max = max_ref[i]
        top = jnp.maximum(jnp.max(scores, axis=0, keepdims=True), tree_max)
        powers = jnp.exp2(scores - top)
        tree = jnp.exp2(tree_max - top)
        scale = live_ref[i] / (jnp.sum(powers, axis=0, keepdims=True) + tree * sum_ref[i])
        delta = scale * (jnp.sum(powers * dweights, axis=0, keepdims=True) + tree * dot_ref[i])
        weights = powers * scale
        dscores = (weights * (dweights - delta)).astype(jnp.bfloat16)
        dscore_ref[i] = dscores
        scale_ref[i] = scale * tree
        delta_ref[i] = delta
        ready.append((weights.astype(jnp.bfloat16), dscores))
    for h in range(heads):
        low = h * HD
        key_sum = value_sum = None
        for b in range(count):
            i = h * count + b
            value_grad = dot(ready[i][0], stage[i][1], NN)
            key_grad = dot(ready[i][1], stage[i][0], NN) * factor
            key_sum = key_grad if b == 0 else key_sum + key_grad
            value_sum = value_grad if b == 0 else value_sum + value_grad
        for i, ref in enumerate(out_refs):
            ref[:, low : low + HD] = key_sum[i * rows : (i + 1) * rows].astype(ref.dtype)
            ref[:, width + low : width + low + HD] = value_sum[i * rows : (i + 1) * rows].astype(
                ref.dtype
            )


def branch_kernel(*refs, parts):
    q_ref, g_ref, bk_ref, power_ref, dweight_ref, dscore_ref, scale_ref, delta_ref = refs[:8]
    pre_refs = refs[8 : 8 + parts]
    dq_ref, dbk_ref, dbv_ref = refs[8 + parts :]
    count, length, _ = q_ref.shape
    heads = bk_ref.shape[2] // HD
    factor = HD**-0.5
    pre = jnp.concatenate([r[:, : heads * HD] for r in pre_refs], axis=0)
    for h in range(heads):
        low = h * HD
        for b in range(count):
            i = h * count + b
            weights = power_ref[i] * scale_ref[i]
            dscores = (weights * (dweight_ref[i] - delta_ref[i])).astype(jnp.bfloat16)
            tree_keys = bk_ref[b, :, low : low + HD]
            value_grad = dot(weights.astype(jnp.bfloat16), head_rows(g_ref, b, h), NN)
            key_grad = dot(dscores, head_rows(q_ref, b, h), NN) * factor
            dbk_ref[b, :, low : low + HD] = key_grad.astype(jnp.bfloat16)
            dbv_ref[b, :, low : low + HD] = value_grad.astype(jnp.bfloat16)
            both = jnp.concatenate([dscore_ref[i], dscores], axis=0)
            keys = jnp.concatenate([pre[:, low : low + HD], tree_keys], axis=0)
            query_grad = (dot(both, keys, TN) * factor).astype(jnp.bfloat16)
            for m in range(PER):
                col = (h * PER + m) * HD
                dq_ref[b, :, col : col + HD] = query_grad[m * length : (m + 1) * length]


def body(
    queries, branch_keys, branch_values, prefix_keys, prefix_values, out_grad, parents, lengths,
    *, groups, branches
):
    count, length, columns = queries.shape
    heads = branch_keys.shape[2] // HD
    prefix = prefix_keys.shape[0] * groups
    packed = jnp.concatenate([prefix_keys, prefix_values], axis=1)
    parts = gather_parts(packed, "group", groups)
    vmem = pl.BlockSpec(memory_space=pltpu.VMEM)
    anywhere = pl.BlockSpec(memory_space=pltpu.HBM)
    hbm = lambda x: pltpu.with_memory_space_constraint(x, pltpu.HBM)
    params = pltpu.CompilerParams(vmem_limit_bytes=16 * 1024 * 1024)
    wide = PER * length
    row = jax.ShapeDtypeStruct((heads * count, 1, wide), jnp.float32)
    block = jax.ShapeDtypeStruct((heads * count, length, wide), jnp.float32)
    like = lambda x: jax.ShapeDtypeStruct(x.shape, x.dtype)
    work = heads * count * wide * HD * 2
    q, g, keys, powers, dweights, tops, sums, dots, live = pl.pallas_call(
        tree_kernel,
        out_shape=[like(queries), like(out_grad), like(branch_keys), block, block, row, row, row, row],
        in_specs=[anywhere] * 4 + [vmem] * 2,
        out_specs=[vmem] * 9,
        scratch_shapes=[
            pltpu.VMEM(branch_values.shape, branch_values.dtype),
            pltpu.SemaphoreType.DMA((2 + 2 * count,)),
        ],
        compiler_params=params,
        cost_estimate=pl.CostEstimate(
            flops=2 * work * length, bytes_accessed=2 * queries.size * 2, transcendentals=wide * length * 4
        ),
        name="tree",
    )(*(hbm(x) for x in (queries, out_grad, branch_keys, branch_values)), parents, lengths.reshape(1, count))
    outs = pl.pallas_call(
        functools.partial(prefix_kernel, parts=groups),
        out_shape=[
            jax.ShapeDtypeStruct((heads * count, prefix, wide), jnp.bfloat16), row, row
        ]
        + [like(packed)] * groups,
        in_specs=[vmem] * (6 + groups),
        out_specs=[vmem] * (3 + groups),
        compiler_params=params,
        cost_estimate=pl.CostEstimate(
            flops=4 * work * prefix, bytes_accessed=0, transcendentals=wide * prefix * 4
        ),
        name="prefix",
    )(q, g, tops, sums, dots, live, *parts)
    query_grad, branch_key_grad, branch_value_grad = pl.pallas_call(
        functools.partial(branch_kernel, parts=groups),
        out_shape=[like(queries), like(branch_keys), like(branch_values)],
        in_specs=[vmem] * (8 + groups),
        out_specs=[vmem] * 3,
        compiler_params=params,
        cost_estimate=pl.CostEstimate(
            flops=4 * work * length, bytes_accessed=queries.size * 2, transcendentals=0
        ),
        name="branch",
    )(q, g, keys, powers, dweights, *outs[:3], *parts)
    owned = scatter_sum(outs[3:], "group", groups)
    total = all_sum(owned, "branch", branches)
    half = prefix_keys.shape[1]
    return query_grad, branch_key_grad, branch_value_grad, total[:, :half], total[:, half:]


def solution(mesh):
    sharded = P(("group", "branch"), None, "head")
    return jax.shard_map(
        functools.partial(body, groups=mesh.shape["group"], branches=mesh.shape["branch"]),
        mesh=mesh,
        in_specs=(
            sharded,
            sharded,
            sharded,
            P("group", "head"),
            P("group", "head"),
            sharded,
            P(("group", "branch"), None),
            P(("group", "branch")),
        ),
        out_specs=(sharded, sharded, sharded, P("group", "head"), P("group", "head")),
        check_vma=False,
    )
```

```python
import functools

import jax
import jax.numpy as jnp
from jax import lax
from jax.experimental import pallas as pl
from jax.experimental.pallas import tpu as pltpu
from jax.sharding import PartitionSpec as P

QH = 32
KVH = 4
HD = 128
PER = QH // KVH
RADIX = 4
GATHER = (3, 2, 1)
SCATTER = (3, 2, 1)
SUM = (3, 2, 1)
LOG2E = 1.4426950408889634
NT = (((1,), (1,)), ((), ()))
NN = (((1,), (0,)), ((), ()))
TN = (((0,), (0,)), ((), ()))


def dot(a, b, dims):
    return lax.dot_general(a, b, dims, preferred_element_type=jnp.float32)


def digits(size):
    out, stride = [], 1
    while stride < size:
        count = min(RADIX, size // stride)
        while (size // stride) % count:
            count -= 1
        if count == 1:
            count = size // stride
        out.append((stride, count))
        stride *= count
    return out


def moved(size, stride, count, step, sign):
    pairs = []
    for i in range(size):
        digit = (i // stride) % count
        if count & (count - 1) == 0:
            other = digit ^ step
        else:
            other = (digit + sign * step) % count
        pairs.append((i, i + (other - digit) * stride))
    return pairs


def in_order(count, order):
    return [step for step in order if step < count] + list(range(len(order) + 1, count))


def exchange(blocks, axis, size, stride, steps, sign):
    count = len(steps) + 1
    return [
        lax.ppermute(block, axis, moved(size, stride, count, step, sign))
        for block, step in zip(blocks, steps)
    ]


def gather_parts(x, axis, size):
    parts = [x]
    for stride, count in digits(size):
        low = len(parts)
        block = x if low == 1 else jnp.stack(parts)
        steps = in_order(count, GATHER)
        for got in exchange([block] * (count - 1), axis, size, stride, steps, 1):
            parts += [got] if low == 1 else [got[i] for i in range(low)]
    return parts


def tree_sum(terms):
    while len(terms) > 1:
        terms = [a + b for a, b in zip(terms[::2], terms[1::2])] + terms[len(terms) & ~1 :]
    return terms[0]


def scatter_sum(parts, axis, size):
    parts, dtype = list(parts), parts[-1].dtype
    for stride, count in reversed(digits(size)):
        low = len(parts) // count
        blocks = parts if low == 1 else [
            jnp.stack(parts[i * low : (i + 1) * low]) for i in range(count)
        ]
        found = dict(zip(in_order(count, GATHER), blocks[1:]))
        steps = in_order(count, SCATTER)
        terms = blocks[:1] + exchange([found[s] for s in steps], axis, size, stride, steps, -1)
        total = tree_sum([t.astype(jnp.float32) for t in terms])
        total = total if low == 1 else total.astype(dtype)
        parts = [total] if low == 1 else [total[i] for i in range(low)]
    return parts[0]


def all_sum(x, axis, size):
    for stride, count in digits(size):
        steps = in_order(count, SUM)
        terms = [x] + exchange([x] * (count - 1), axis, size, stride, steps, 1)
        x = tree_sum([t.astype(jnp.float32) for t in terms]).astype(x.dtype)
    return x


def head_rows(ref, b, h):
    cols = [slice((h * PER + m) * HD, (h * PER + m + 1) * HD) for m in range(PER)]
    return jnp.concatenate([ref[b, :, c] for c in cols], axis=0)


def tree_kernel(
    q_hbm, g_hbm, bk_hbm, bv_hbm, par_ref, len_ref,
    q_ref, g_ref, bk_ref, power_ref, dweight_ref, max_ref, sum_ref, dot_ref, live_ref,
    bv_ref, sems,
):
    count, length, _ = q_ref.shape
    heads = bk_ref.shape[2] // HD
    pairs = [(q_hbm.at[0], q_ref.at[0]), (g_hbm.at[0], g_ref.at[0])]
    pairs += [(bk_hbm, bk_ref), (bv_hbm, bv_ref)]
    for b in range(1, count):
        pairs += [(q_hbm.at[b], q_ref.at[b]), (g_hbm.at[b], g_ref.at[b])]
    copies = [pltpu.make_async_copy(s, d, sems.at[i]) for i, (s, d) in enumerate(pairs)]
    for copy in copies:
        copy.start()
    slot = lax.broadcasted_iota(jnp.int32, (length, length), 0)
    token = lax.broadcasted_iota(jnp.int32, (length, length), 1)
    reaches = []
    for b in range(count):
        hit = (slot == token) | (slot == par_ref[b : b + 1, :])
        reaches.append(hit.astype(jnp.float32).astype(jnp.bfloat16))
    for rounds in range((length - 1).bit_length()):
        reaches = [jnp.minimum(dot(r, r, NN), 1.0).astype(jnp.bfloat16) for r in reaches]
    masks = [jnp.concatenate([r.astype(jnp.float32)] * PER, axis=1) > 0.5 for r in reaches]
    place = lax.broadcasted_iota(jnp.int32, (1, PER * length), 1) % length
    for b in range(count):
        for copy in copies[2 * b + 2 if b else 0 : 2 * b + 4]:
            copy.wait()
        stage = []
        for h in range(heads):
            cols = slice(h * HD, (h + 1) * HD)
            stage.append((
                dot(bk_ref[b, :, cols], head_rows(q_ref, b, h), NT),
                dot(bv_ref[b, :, cols], head_rows(g_ref, b, h), NT),
            ))
        live = (place < len_ref[:, b : b + 1]).astype(jnp.float32)
        for h, (scores, dweights) in enumerate(stage):
            i = h * count + b
            scores = jnp.where(masks[b], scores * (HD**-0.5 * LOG2E), -1e30)
            top = jnp.max(scores, axis=0, keepdims=True)
            powers = jnp.exp2(scores - top)
            power_ref[i] = powers
            dweight_ref[i] = dweights
            live_ref[i] = live
            max_ref[i] = top
            sum_ref[i] = jnp.sum(powers, axis=0, keepdims=True)
            dot_ref[i] = jnp.sum(powers * dweights, axis=0, keepdims=True)


def prefix_kernel(*refs, parts):
    q_ref, g_ref, max_ref, sum_ref, dot_ref, live_ref = refs[:6]
    pre_refs = refs[6 : 6 + parts]
    dscore_ref, scale_ref, delta_ref = refs[6 + parts : 9 + parts]
    out_refs = refs[9 + parts :]
    count, length, _ = q_ref.shape
    rows, width = pre_refs[0].shape
    width //= 2
    heads = width // HD
    factor = HD**-0.5
    pre = jnp.concatenate([r[...] for r in pre_refs], axis=0)
    stage = []
    for h in range(heads):
        low = h * HD
        keys = pre[:, low : low + HD]
        values = pre[:, width + low : width + low + HD]
        for b in range(count):
            q = head_rows(q_ref, b, h)
            g = head_rows(g_ref, b, h)
            stage.append((q, g, dot(keys, q, NT), dot(values, g, NT)))
    ready = []
    for i, (q, g, scores, dweights) in enumerate(stage):
        scores = scores * (factor * LOG2E)
        tree_max = max_ref[i]
        top = jnp.maximum(jnp.max(scores, axis=0, keepdims=True), tree_max)
        powers = jnp.exp2(scores - top)
        tree = jnp.exp2(tree_max - top)
        scale = live_ref[i] / (jnp.sum(powers, axis=0, keepdims=True) + tree * sum_ref[i])
        delta = scale * (jnp.sum(powers * dweights, axis=0, keepdims=True) + tree * dot_ref[i])
        weights = powers * scale
        dscores = (weights * (dweights - delta)).astype(jnp.bfloat16)
        dscore_ref[i] = dscores
        scale_ref[i] = scale * tree
        delta_ref[i] = delta
        ready.append((weights.astype(jnp.bfloat16), dscores))
    for h in range(heads):
        low = h * HD
        key_sum = value_sum = None
        for b in range(count):
            i = h * count + b
            value_grad = dot(ready[i][0], stage[i][1], NN)
            key_grad = dot(ready[i][1], stage[i][0], NN) * factor
            key_sum = key_grad if b == 0 else key_sum + key_grad
            value_sum = value_grad if b == 0 else value_sum + value_grad
        for i, ref in enumerate(out_refs):
            ref[:, low : low + HD] = key_sum[i * rows : (i + 1) * rows].astype(ref.dtype)
            ref[:, width + low : width + low + HD] = value_sum[i * rows : (i + 1) * rows].astype(
                ref.dtype
            )


def branch_kernel(*refs, parts):
    q_ref, g_ref, bk_ref, power_ref, dweight_ref, dscore_ref, scale_ref, delta_ref = refs[:8]
    pre_refs = refs[8 : 8 + parts]
    dq_ref, dbk_ref, dbv_ref = refs[8 + parts :]
    count, length, _ = q_ref.shape
    heads = bk_ref.shape[2] // HD
    factor = HD**-0.5
    pre = jnp.concatenate([r[:, : heads * HD] for r in pre_refs], axis=0)
    for h in range(heads):
        low = h * HD
        for b in range(count):
            i = h * count + b
            weights = power_ref[i] * scale_ref[i]
            dscores = (weights * (dweight_ref[i] - delta_ref[i])).astype(jnp.bfloat16)
            tree_keys = bk_ref[b, :, low : low + HD]
            value_grad = dot(weights.astype(jnp.bfloat16), head_rows(g_ref, b, h), NN)
            key_grad = dot(dscores, head_rows(q_ref, b, h), NN) * factor
            dbk_ref[b, :, low : low + HD] = key_grad.astype(jnp.bfloat16)
            dbv_ref[b, :, low : low + HD] = value_grad.astype(jnp.bfloat16)
            both = jnp.concatenate([dscore_ref[i], dscores], axis=0)
            keys = jnp.concatenate([pre[:, low : low + HD], tree_keys], axis=0)
            query_grad = (dot(both, keys, TN) * factor).astype(jnp.bfloat16)
            for m in range(PER):
                col = (h * PER + m) * HD
                dq_ref[b, :, col : col + HD] = query_grad[m * length : (m + 1) * length]


def body(
    queries, branch_keys, branch_values, prefix_keys, prefix_values, out_grad, parents, lengths,
    *, groups, branches
):
    count, length, columns = queries.shape
    heads = branch_keys.shape[2] // HD
    prefix = prefix_keys.shape[0] * groups
    packed = jnp.concatenate([prefix_keys, prefix_values], axis=1)
    parts = gather_parts(packed, "group", groups)
    vmem = pl.BlockSpec(memory_space=pltpu.VMEM)
    anywhere = pl.BlockSpec(memory_space=pltpu.HBM)
    hbm = lambda x: pltpu.with_memory_space_constraint(x, pltpu.HBM)
    params = pltpu.CompilerParams(vmem_limit_bytes=16 * 1024 * 1024)
    wide = PER * length
    row = jax.ShapeDtypeStruct((heads * count, 1, wide), jnp.float32)
    block = jax.ShapeDtypeStruct((heads * count, length, wide), jnp.float32)
    like = lambda x: jax.ShapeDtypeStruct(x.shape, x.dtype)
    work = heads * count * wide * HD * 2
    q, g, keys, powers, dweights, tops, sums, dots, live = pl.pallas_call(
        tree_kernel,
        out_shape=[like(queries), like(out_grad), like(branch_keys), block, block, row, row, row, row],
        in_specs=[anywhere] * 4 + [vmem] * 2,
        out_specs=[vmem] * 9,
        scratch_shapes=[
            pltpu.VMEM(branch_values.shape, branch_values.dtype),
            pltpu.SemaphoreType.DMA((2 + 2 * count,)),
        ],
        compiler_params=params,
        cost_estimate=pl.CostEstimate(
            flops=2 * work * length, bytes_accessed=2 * queries.size * 2, transcendentals=wide * length * 4
        ),
        name="tree",
    )(*(hbm(x) for x in (queries, out_grad, branch_keys, branch_values)), parents, lengths.reshape(1, count))
    outs = pl.pallas_call(
        functools.partial(prefix_kernel, parts=groups),
        out_shape=[
            jax.ShapeDtypeStruct((heads * count, prefix, wide), jnp.bfloat16), row, row
        ]
        + [jax.ShapeDtypeStruct(packed.shape, jnp.float32)]
        + [like(packed)] * (groups - 1),
        in_specs=[vmem] * (6 + groups),
        out_specs=[vmem] * (3 + groups),
        compiler_params=params,
        cost_estimate=pl.CostEstimate(
            flops=4 * work * prefix, bytes_accessed=0, transcendentals=wide * prefix * 4
        ),
        name="prefix",
    )(q, g, tops, sums, dots, live, *parts)
    query_grad, branch_key_grad, branch_value_grad = pl.pallas_call(
        functools.partial(branch_kernel, parts=groups),
        out_shape=[like(queries), like(branch_keys), like(branch_values)],
        in_specs=[vmem] * (8 + groups),
        out_specs=[vmem] * 3,
        compiler_params=params,
        cost_estimate=pl.CostEstimate(
            flops=4 * work * length, bytes_accessed=queries.size * 2, transcendentals=0
        ),
        name="branch",
    )(q, g, keys, powers, dweights, *outs[:3], *parts)
    owned = scatter_sum(outs[3:], "group", groups)
    total = all_sum(owned, "branch", branches)
    total = total.astype(jnp.bfloat16)
    half = prefix_keys.shape[1]
    return query_grad, branch_key_grad, branch_value_grad, total[:, :half], total[:, half:]


def solution(mesh):
    sharded = P(("group", "branch"), None, "head")
    return jax.shard_map(
        functools.partial(body, groups=mesh.shape["group"], branches=mesh.shape["branch"]),
        mesh=mesh,
        in_specs=(
            sharded,
            sharded,
            sharded,
            P("group", "head"),
            P("group", "head"),
            sharded,
            P(("group", "branch"), None),
            P(("group", "branch")),
        ),
        out_specs=(sharded, sharded, sharded, P("group", "head"), P("group", "head")),
        check_vma=False,
    )
```

```python
import functools

import jax
import jax.numpy as jnp
from jax import lax
from jax.experimental import pallas as pl
from jax.experimental.pallas import tpu as pltpu
from jax.sharding import PartitionSpec as P

QH = 32
KVH = 4
HD = 128
PER = QH // KVH
RADIX = 4
GATHER = (3, 2, 1)
SCATTER = (3, 2, 1)
SUM = (3, 2, 1)
LOG2E = 1.4426950408889634
NT = (((1,), (1,)), ((), ()))
NN = (((1,), (0,)), ((), ()))
TN = (((0,), (0,)), ((), ()))


def dot(a, b, dims):
    return lax.dot_general(a, b, dims, preferred_element_type=jnp.float32)


def digits(size):
    out, stride = [], 1
    while stride < size:
        count = min(RADIX, size // stride)
        while (size // stride) % count:
            count -= 1
        if count == 1:
            count = size // stride
        out.append((stride, count))
        stride *= count
    return out


def moved(size, stride, count, step, sign):
    pairs = []
    for i in range(size):
        digit = (i // stride) % count
        if count & (count - 1) == 0:
            other = digit ^ step
        else:
            other = (digit + sign * step) % count
        pairs.append((i, i + (other - digit) * stride))
    return pairs


def in_order(count, order):
    return [step for step in order if step < count] + list(range(len(order) + 1, count))


def exchange(blocks, axis, size, stride, steps, sign):
    count = len(steps) + 1
    return [
        lax.ppermute(block, axis, moved(size, stride, count, step, sign))
        for block, step in zip(blocks, steps)
    ]


def gather_parts(x, axis, size):
    parts = [x]
    for stride, count in digits(size):
        low = len(parts)
        block = x if low == 1 else jnp.stack(parts)
        steps = in_order(count, GATHER)
        for got in exchange([block] * (count - 1), axis, size, stride, steps, 1):
            parts += [got] if low == 1 else [got[i] for i in range(low)]
    return parts


def tree_sum(terms):
    while len(terms) > 1:
        terms = [a + b for a, b in zip(terms[::2], terms[1::2])] + terms[len(terms) & ~1 :]
    return terms[0]


def scatter_sum(parts, axis, size):
    parts = list(parts)
    for stride, count in reversed(digits(size)):
        low = len(parts) // count
        blocks = parts if low == 1 else [
            jnp.stack(parts[i * low : (i + 1) * low]) for i in range(count)
        ]
        found = dict(zip(in_order(count, GATHER), blocks[1:]))
        steps = in_order(count, SCATTER)
        terms = blocks[:1] + exchange([found[s] for s in steps], axis, size, stride, steps, -1)
        total = tree_sum([t.astype(jnp.float32) for t in terms])
        parts = [total] if low == 1 else [total[i] for i in range(low)]
    return parts[0]


def all_sum(x, axis, size):
    for stride, count in digits(size):
        steps = in_order(count, SUM)
        x = tree_sum([x] + exchange([x] * (count - 1), axis, size, stride, steps, 1))
    return x


def head_rows(ref, b, h):
    cols = [slice((h * PER + m) * HD, (h * PER + m + 1) * HD) for m in range(PER)]
    return jnp.concatenate([ref[b, :, c] for c in cols], axis=0)


def tree_kernel(
    q_hbm, g_hbm, bk_hbm, bv_hbm, par_ref, len_ref,
    q_ref, g_ref, bk_ref, power_ref, dweight_ref, max_ref, sum_ref, dot_ref, live_ref,
    bv_ref, sems,
):
    count, length, _ = q_ref.shape
    heads = bk_ref.shape[2] // HD
    pairs = [(q_hbm.at[0], q_ref.at[0]), (g_hbm.at[0], g_ref.at[0])]
    pairs += [(bk_hbm, bk_ref), (bv_hbm, bv_ref)]
    for b in range(1, count):
        pairs += [(q_hbm.at[b], q_ref.at[b]), (g_hbm.at[b], g_ref.at[b])]
    copies = [pltpu.make_async_copy(s, d, sems.at[i]) for i, (s, d) in enumerate(pairs)]
    for copy in copies:
        copy.start()
    slot = lax.broadcasted_iota(jnp.int32, (length, length), 0)
    token = lax.broadcasted_iota(jnp.int32, (length, length), 1)
    reaches = []
    for b in range(count):
        hit = (slot == token) | (slot == par_ref[b : b + 1, :])
        reaches.append(hit.astype(jnp.float32).astype(jnp.bfloat16))
    for rounds in range((length - 1).bit_length()):
        reaches = [jnp.minimum(dot(r, r, NN), 1.0).astype(jnp.bfloat16) for r in reaches]
    masks = [jnp.concatenate([r.astype(jnp.float32)] * PER, axis=1) > 0.5 for r in reaches]
    place = lax.broadcasted_iota(jnp.int32, (1, PER * length), 1) % length
    for b in range(count):
        for copy in copies[2 * b + 2 if b else 0 : 2 * b + 4]:
            copy.wait()
        stage = []
        for h in range(heads):
            cols = slice(h * HD, (h + 1) * HD)
            stage.append((
                dot(bk_ref[b, :, cols], head_rows(q_ref, b, h), NT),
                dot(bv_ref[b, :, cols], head_rows(g_ref, b, h), NT),
            ))
        live = (place < len_ref[:, b : b + 1]).astype(jnp.float32)
        for h, (scores, dweights) in enumerate(stage):
            i = h * count + b
            scores = jnp.where(masks[b], scores * (HD**-0.5 * LOG2E), -1e30)
            top = jnp.max(scores, axis=0, keepdims=True)
            powers = jnp.exp2(scores - top)
            power_ref[i] = powers
            dweight_ref[i] = dweights
            live_ref[i] = live
            max_ref[i] = top
            sum_ref[i] = jnp.sum(powers, axis=0, keepdims=True)
            dot_ref[i] = jnp.sum(powers * dweights, axis=0, keepdims=True)


def prefix_kernel(*refs, parts):
    q_ref, g_ref, max_ref, sum_ref, dot_ref, live_ref = refs[:6]
    pre_refs = refs[6 : 6 + parts]
    dscore_ref, scale_ref, delta_ref = refs[6 + parts : 9 + parts]
    out_refs = refs[9 + parts :]
    count, length, _ = q_ref.shape
    rows, width = pre_refs[0].shape
    width //= 2
    heads = width // HD
    factor = HD**-0.5
    pre = jnp.concatenate([r[...] for r in pre_refs], axis=0)
    stage = []
    for h in range(heads):
        low = h * HD
        keys = pre[:, low : low + HD]
        values = pre[:, width + low : width + low + HD]
        for b in range(count):
            q = head_rows(q_ref, b, h)
            g = head_rows(g_ref, b, h)
            stage.append((q, g, dot(keys, q, NT), dot(values, g, NT)))
    ready = []
    for i, (q, g, scores, dweights) in enumerate(stage):
        scores = scores * (factor * LOG2E)
        tree_max = max_ref[i]
        top = jnp.maximum(jnp.max(scores, axis=0, keepdims=True), tree_max)
        powers = jnp.exp2(scores - top)
        tree = jnp.exp2(tree_max - top)
        scale = live_ref[i] / (jnp.sum(powers, axis=0, keepdims=True) + tree * sum_ref[i])
        delta = scale * (jnp.sum(powers * dweights, axis=0, keepdims=True) + tree * dot_ref[i])
        weights = powers * scale
        dscores = (weights * (dweights - delta)).astype(jnp.bfloat16)
        dscore_ref[i] = dscores
        scale_ref[i] = scale * tree
        delta_ref[i] = delta
        ready.append((weights.astype(jnp.bfloat16), dscores))
    for h in range(heads):
        low = h * HD
        key_sum = value_sum = None
        for b in range(count):
            i = h * count + b
            value_grad = dot(ready[i][0], stage[i][1], NN)
            key_grad = dot(ready[i][1], stage[i][0], NN) * factor
            key_sum = key_grad if b == 0 else key_sum + key_grad
            value_sum = value_grad if b == 0 else value_sum + value_grad
        for i, ref in enumerate(out_refs):
            ref[:, low : low + HD] = key_sum[i * rows : (i + 1) * rows].astype(ref.dtype)
            ref[:, width + low : width + low + HD] = value_sum[i * rows : (i + 1) * rows].astype(
                ref.dtype
            )


def branch_kernel(*refs, parts):
    q_ref, g_ref, bk_ref, power_ref, dweight_ref, dscore_ref, scale_ref, delta_ref = refs[:8]
    pre_refs = refs[8 : 8 + parts]
    dq_ref, dbk_ref, dbv_ref = refs[8 + parts :]
    count, length, _ = q_ref.shape
    heads = bk_ref.shape[2] // HD
    factor = HD**-0.5
    pre = jnp.concatenate([r[:, : heads * HD] for r in pre_refs], axis=0)
    for h in range(heads):
        low = h * HD
        for b in range(count):
            i = h * count + b
            weights = power_ref[i] * scale_ref[i]
            dscores = (weights * (dweight_ref[i] - delta_ref[i])).astype(jnp.bfloat16)
            tree_keys = bk_ref[b, :, low : low + HD]
            value_grad = dot(weights.astype(jnp.bfloat16), head_rows(g_ref, b, h), NN)
            key_grad = dot(dscores, head_rows(q_ref, b, h), NN) * factor
            dbk_ref[b, :, low : low + HD] = key_grad.astype(jnp.bfloat16)
            dbv_ref[b, :, low : low + HD] = value_grad.astype(jnp.bfloat16)
            both = jnp.concatenate([dscore_ref[i], dscores], axis=0)
            keys = jnp.concatenate([pre[:, low : low + HD], tree_keys], axis=0)
            query_grad = (dot(both, keys, TN) * factor).astype(jnp.bfloat16)
            for m in range(PER):
                col = (h * PER + m) * HD
                dq_ref[b, :, col : col + HD] = query_grad[m * length : (m + 1) * length]


def body(
    queries, branch_keys, branch_values, prefix_keys, prefix_values, out_grad, parents, lengths,
    *, groups, branches
):
    count, length, columns = queries.shape
    heads = branch_keys.shape[2] // HD
    prefix = prefix_keys.shape[0] * groups
    packed = jnp.concatenate([prefix_keys, prefix_values], axis=1)
    parts = gather_parts(packed, "group", groups)
    vmem = pl.BlockSpec(memory_space=pltpu.VMEM)
    anywhere = pl.BlockSpec(memory_space=pltpu.HBM)
    hbm = lambda x: pltpu.with_memory_space_constraint(x, pltpu.HBM)
    params = pltpu.CompilerParams(vmem_limit_bytes=16 * 1024 * 1024)
    wide = PER * length
    row = jax.ShapeDtypeStruct((heads * count, 1, wide), jnp.float32)
    block = jax.ShapeDtypeStruct((heads * count, length, wide), jnp.float32)
    like = lambda x: jax.ShapeDtypeStruct(x.shape, x.dtype)
    work = heads * count * wide * HD * 2
    q, g, keys, powers, dweights, tops, sums, dots, live = pl.pallas_call(
        tree_kernel,
        out_shape=[like(queries), like(out_grad), like(branch_keys), block, block, row, row, row, row],
        in_specs=[anywhere] * 4 + [vmem] * 2,
        out_specs=[vmem] * 9,
        scratch_shapes=[
            pltpu.VMEM(branch_values.shape, branch_values.dtype),
            pltpu.SemaphoreType.DMA((2 + 2 * count,)),
        ],
        compiler_params=params,
        cost_estimate=pl.CostEstimate(
            flops=2 * work * length, bytes_accessed=2 * queries.size * 2, transcendentals=wide * length * 4
        ),
        name="tree",
    )(*(hbm(x) for x in (queries, out_grad, branch_keys, branch_values)), parents, lengths.reshape(1, count))
    outs = pl.pallas_call(
        functools.partial(prefix_kernel, parts=groups),
        out_shape=[
            jax.ShapeDtypeStruct((heads * count, prefix, wide), jnp.bfloat16), row, row
        ]
        + [jax.ShapeDtypeStruct(packed.shape, jnp.float32)] * (groups - 1)
        + [like(packed)],
        in_specs=[vmem] * (6 + groups),
        out_specs=[vmem] * (3 + groups),
        compiler_params=params,
        cost_estimate=pl.CostEstimate(
            flops=4 * work * prefix, bytes_accessed=0, transcendentals=wide * prefix * 4
        ),
        name="prefix",
    )(q, g, tops, sums, dots, live, *parts)
    query_grad, branch_key_grad, branch_value_grad = pl.pallas_call(
        functools.partial(branch_kernel, parts=groups),
        out_shape=[like(queries), like(branch_keys), like(branch_values)],
        in_specs=[vmem] * (8 + groups),
        out_specs=[vmem] * 3,
        compiler_params=params,
        cost_estimate=pl.CostEstimate(
            flops=4 * work * length, bytes_accessed=queries.size * 2, transcendentals=0
        ),
        name="branch",
    )(q, g, keys, powers, dweights, *outs[:3], *parts)
    owned = scatter_sum(outs[3:], "group", groups)
    total = all_sum(owned, "branch", branches)
    total = total.astype(jnp.bfloat16)
    half = prefix_keys.shape[1]
    return query_grad, branch_key_grad, branch_value_grad, total[:, :half], total[:, half:]


def solution(mesh):
    sharded = P(("group", "branch"), None, "head")
    return jax.shard_map(
        functools.partial(body, groups=mesh.shape["group"], branches=mesh.shape["branch"]),
        mesh=mesh,
        in_specs=(
            sharded,
            sharded,
            sharded,
            P("group", "head"),
            P("group", "head"),
            sharded,
            P(("group", "branch"), None),
            P(("group", "branch")),
        ),
        out_specs=(sharded, sharded, sharded, P("group", "head"), P("group", "head")),
        check_vma=False,
    )
```

```python
import functools

import jax
import jax.numpy as jnp
from jax import lax
from jax.experimental import pallas as pl
from jax.experimental.pallas import tpu as pltpu
from jax.sharding import PartitionSpec as P

QH = 32
KVH = 4
HD = 128
PER = QH // KVH
RADIX = 4
GATHER = (3, 2, 1)
SCATTER = (3, 2, 1)
SUM = (3, 2, 1)
LOG2E = 1.4426950408889634
NT = (((1,), (1,)), ((), ()))
NN = (((1,), (0,)), ((), ()))
TN = (((0,), (0,)), ((), ()))


def dot(a, b, dims):
    return lax.dot_general(a, b, dims, preferred_element_type=jnp.float32)


def digits(size):
    out, stride = [], 1
    while stride < size:
        count = min(RADIX, size // stride)
        while (size // stride) % count:
            count -= 1
        if count == 1:
            count = size // stride
        out.append((stride, count))
        stride *= count
    return out


def moved(size, stride, count, step, sign):
    pairs = []
    for i in range(size):
        digit = (i // stride) % count
        if count & (count - 1) == 0:
            other = digit ^ step
        else:
            other = (digit + sign * step) % count
        pairs.append((i, i + (other - digit) * stride))
    return pairs


def in_order(count, order):
    return [step for step in order if step < count] + list(range(len(order) + 1, count))


def exchange(blocks, axis, size, stride, steps, sign):
    count = len(steps) + 1
    return [
        lax.ppermute(block, axis, moved(size, stride, count, step, sign))
        for block, step in zip(blocks, steps)
    ]


def gather_parts(x, axis, size):
    parts = [x]
    for stride, count in digits(size):
        low = len(parts)
        block = x if low == 1 else jnp.stack(parts)
        steps = in_order(count, GATHER)
        for got in exchange([block] * (count - 1), axis, size, stride, steps, 1):
            parts += [got] if low == 1 else [got[i] for i in range(low)]
    return parts


def tree_sum(terms):
    while len(terms) > 1:
        terms = [a + b for a, b in zip(terms[::2], terms[1::2])] + terms[len(terms) & ~1 :]
    return terms[0]


def scatter_sum(parts, axis, size):
    parts = list(parts)
    for stride, count in reversed(digits(size)):
        low = len(parts) // count
        blocks = parts if low == 1 else [
            jnp.stack(parts[i * low : (i + 1) * low]) for i in range(count)
        ]
        found = dict(zip(in_order(count, GATHER), blocks[1:]))
        steps = in_order(count, SCATTER)
        terms = blocks[:1] + exchange([found[s] for s in steps], axis, size, stride, steps, -1)
        total = tree_sum([t.astype(jnp.float32) for t in terms])
        parts = [total] if low == 1 else [total[i] for i in range(low)]
    return parts[0]


def all_sum(x, axis, size):
    for stride, count in digits(size):
        steps = in_order(count, SUM)
        sent = x.astype(jnp.bfloat16)
        terms = [sent] + exchange([sent] * (count - 1), axis, size, stride, steps, 1)
        x = tree_sum([t.astype(jnp.float32) for t in terms])
    return x


def head_rows(ref, b, h):
    cols = [slice((h * PER + m) * HD, (h * PER + m + 1) * HD) for m in range(PER)]
    return jnp.concatenate([ref[b, :, c] for c in cols], axis=0)


def tree_kernel(
    q_hbm, g_hbm, bk_hbm, bv_hbm, par_ref, len_ref,
    q_ref, g_ref, bk_ref, power_ref, dweight_ref, max_ref, sum_ref, dot_ref, live_ref,
    bv_ref, sems,
):
    count, length, _ = q_ref.shape
    heads = bk_ref.shape[2] // HD
    pairs = [(q_hbm.at[0], q_ref.at[0]), (g_hbm.at[0], g_ref.at[0])]
    pairs += [(bk_hbm, bk_ref), (bv_hbm, bv_ref)]
    for b in range(1, count):
        pairs += [(q_hbm.at[b], q_ref.at[b]), (g_hbm.at[b], g_ref.at[b])]
    copies = [pltpu.make_async_copy(s, d, sems.at[i]) for i, (s, d) in enumerate(pairs)]
    for copy in copies:
        copy.start()
    slot = lax.broadcasted_iota(jnp.int32, (length, length), 0)
    token = lax.broadcasted_iota(jnp.int32, (length, length), 1)
    reaches = []
    for b in range(count):
        hit = (slot == token) | (slot == par_ref[b : b + 1, :])
        reaches.append(hit.astype(jnp.float32).astype(jnp.bfloat16))
    for rounds in range((length - 1).bit_length()):
        reaches = [jnp.minimum(dot(r, r, NN), 1.0).astype(jnp.bfloat16) for r in reaches]
    masks = [jnp.concatenate([r.astype(jnp.float32)] * PER, axis=1) > 0.5 for r in reaches]
    place = lax.broadcasted_iota(jnp.int32, (1, PER * length), 1) % length
    for b in range(count):
        for copy in copies[2 * b + 2 if b else 0 : 2 * b + 4]:
            copy.wait()
        stage = []
        for h in range(heads):
            cols = slice(h * HD, (h + 1) * HD)
            stage.append((
                dot(bk_ref[b, :, cols], head_rows(q_ref, b, h), NT),
                dot(bv_ref[b, :, cols], head_rows(g_ref, b, h), NT),
            ))
        live = (place < len_ref[:, b : b + 1]).astype(jnp.float32)
        for h, (scores, dweights) in enumerate(stage):
            i = h * count + b
            scores = jnp.where(masks[b], scores * (HD**-0.5 * LOG2E), -1e30)
            top = jnp.max(scores, axis=0, keepdims=True)
            powers = jnp.exp2(scores - top)
            power_ref[i] = powers
            dweight_ref[i] = dweights
            live_ref[i] = live
            max_ref[i] = top
            sum_ref[i] = jnp.sum(powers, axis=0, keepdims=True)
            dot_ref[i] = jnp.sum(powers * dweights, axis=0, keepdims=True)


def prefix_kernel(*refs, parts):
    q_ref, g_ref, max_ref, sum_ref, dot_ref, live_ref = refs[:6]
    pre_refs = refs[6 : 6 + parts]
    dscore_ref, scale_ref, delta_ref = refs[6 + parts : 9 + parts]
    out_refs = refs[9 + parts :]
    count, length, _ = q_ref.shape
    rows, width = pre_refs[0].shape
    width //= 2
    heads = width // HD
    factor = HD**-0.5
    pre = jnp.concatenate([r[...] for r in pre_refs], axis=0)
    stage = []
    for h in range(heads):
        low = h * HD
        keys = pre[:, low : low + HD]
        values = pre[:, width + low : width + low + HD]
        for b in range(count):
            q = head_rows(q_ref, b, h)
            g = head_rows(g_ref, b, h)
            stage.append((q, g, dot(keys, q, NT), dot(values, g, NT)))
    ready = []
    for i, (q, g, scores, dweights) in enumerate(stage):
        scores = scores * (factor * LOG2E)
        tree_max = max_ref[i]
        top = jnp.maximum(jnp.max(scores, axis=0, keepdims=True), tree_max)
        powers = jnp.exp2(scores - top)
        tree = jnp.exp2(tree_max - top)
        scale = live_ref[i] / (jnp.sum(powers, axis=0, keepdims=True) + tree * sum_ref[i])
        delta = scale * (jnp.sum(powers * dweights, axis=0, keepdims=True) + tree * dot_ref[i])
        weights = powers * scale
        dscores = (weights * (dweights - delta)).astype(jnp.bfloat16)
        dscore_ref[i] = dscores
        scale_ref[i] = scale * tree
        delta_ref[i] = delta
        ready.append((weights.astype(jnp.bfloat16), dscores))
    for h in range(heads):
        low = h * HD
        key_sum = value_sum = None
        for b in range(count):
            i = h * count + b
            value_grad = dot(ready[i][0], stage[i][1], NN)
            key_grad = dot(ready[i][1], stage[i][0], NN) * factor
            key_sum = key_grad if b == 0 else key_sum + key_grad
            value_sum = value_grad if b == 0 else value_sum + value_grad
        for i, ref in enumerate(out_refs):
            ref[:, low : low + HD] = key_sum[i * rows : (i + 1) * rows].astype(ref.dtype)
            ref[:, width + low : width + low + HD] = value_sum[i * rows : (i + 1) * rows].astype(
                ref.dtype
            )


def branch_kernel(*refs, parts):
    q_ref, g_ref, bk_ref, power_ref, dweight_ref, dscore_ref, scale_ref, delta_ref = refs[:8]
    pre_refs = refs[8 : 8 + parts]
    dq_ref, dbk_ref, dbv_ref = refs[8 + parts :]
    count, length, _ = q_ref.shape
    heads = bk_ref.shape[2] // HD
    factor = HD**-0.5
    pre = jnp.concatenate([r[:, : heads * HD] for r in pre_refs], axis=0)
    for h in range(heads):
        low = h * HD
        for b in range(count):
            i = h * count + b
            weights = power_ref[i] * scale_ref[i]
            dscores = (weights * (dweight_ref[i] - delta_ref[i])).astype(jnp.bfloat16)
            tree_keys = bk_ref[b, :, low : low + HD]
            value_grad = dot(weights.astype(jnp.bfloat16), head_rows(g_ref, b, h), NN)
            key_grad = dot(dscores, head_rows(q_ref, b, h), NN) * factor
            dbk_ref[b, :, low : low + HD] = key_grad.astype(jnp.bfloat16)
            dbv_ref[b, :, low : low + HD] = value_grad.astype(jnp.bfloat16)
            both = jnp.concatenate([dscore_ref[i], dscores], axis=0)
            keys = jnp.concatenate([pre[:, low : low + HD], tree_keys], axis=0)
            query_grad = (dot(both, keys, TN) * factor).astype(jnp.bfloat16)
            for m in range(PER):
                col = (h * PER + m) * HD
                dq_ref[b, :, col : col + HD] = query_grad[m * length : (m + 1) * length]


def body(
    queries, branch_keys, branch_values, prefix_keys, prefix_values, out_grad, parents, lengths,
    *, groups, branches
):
    count, length, columns = queries.shape
    heads = branch_keys.shape[2] // HD
    prefix = prefix_keys.shape[0] * groups
    packed = jnp.concatenate([prefix_keys, prefix_values], axis=1)
    parts = gather_parts(packed, "group", groups)
    vmem = pl.BlockSpec(memory_space=pltpu.VMEM)
    anywhere = pl.BlockSpec(memory_space=pltpu.HBM)
    hbm = lambda x: pltpu.with_memory_space_constraint(x, pltpu.HBM)
    params = pltpu.CompilerParams(vmem_limit_bytes=16 * 1024 * 1024)
    wide = PER * length
    row = jax.ShapeDtypeStruct((heads * count, 1, wide), jnp.float32)
    block = jax.ShapeDtypeStruct((heads * count, length, wide), jnp.float32)
    like = lambda x: jax.ShapeDtypeStruct(x.shape, x.dtype)
    work = heads * count * wide * HD * 2
    q, g, keys, powers, dweights, tops, sums, dots, live = pl.pallas_call(
        tree_kernel,
        out_shape=[like(queries), like(out_grad), like(branch_keys), block, block, row, row, row, row],
        in_specs=[anywhere] * 4 + [vmem] * 2,
        out_specs=[vmem] * 9,
        scratch_shapes=[
            pltpu.VMEM(branch_values.shape, branch_values.dtype),
            pltpu.SemaphoreType.DMA((2 + 2 * count,)),
        ],
        compiler_params=params,
        cost_estimate=pl.CostEstimate(
            flops=2 * work * length, bytes_accessed=2 * queries.size * 2, transcendentals=wide * length * 4
        ),
        name="tree",
    )(*(hbm(x) for x in (queries, out_grad, branch_keys, branch_values)), parents, lengths.reshape(1, count))
    outs = pl.pallas_call(
        functools.partial(prefix_kernel, parts=groups),
        out_shape=[
            jax.ShapeDtypeStruct((heads * count, prefix, wide), jnp.bfloat16), row, row
        ]
        + [jax.ShapeDtypeStruct(packed.shape, jnp.float32)]
        + [like(packed)] * (groups - 1),
        in_specs=[vmem] * (6 + groups),
        out_specs=[vmem] * (3 + groups),
        compiler_params=params,
        cost_estimate=pl.CostEstimate(
            flops=4 * work * prefix, bytes_accessed=0, transcendentals=wide * prefix * 4
        ),
        name="prefix",
    )(q, g, tops, sums, dots, live, *parts)
    query_grad, branch_key_grad, branch_value_grad = pl.pallas_call(
        functools.partial(branch_kernel, parts=groups),
        out_shape=[like(queries), like(branch_keys), like(branch_values)],
        in_specs=[vmem] * (8 + groups),
        out_specs=[vmem] * 3,
        compiler_params=params,
        cost_estimate=pl.CostEstimate(
            flops=4 * work * length, bytes_accessed=queries.size * 2, transcendentals=0
        ),
        name="branch",
    )(q, g, keys, powers, dweights, *outs[:3], *parts)
    owned = scatter_sum(outs[3:], "group", groups)
    total = all_sum(owned, "branch", branches)
    total = total.astype(jnp.bfloat16)
    half = prefix_keys.shape[1]
    return query_grad, branch_key_grad, branch_value_grad, total[:, :half], total[:, half:]


def solution(mesh):
    sharded = P(("group", "branch"), None, "head")
    return jax.shard_map(
        functools.partial(body, groups=mesh.shape["group"], branches=mesh.shape["branch"]),
        mesh=mesh,
        in_specs=(
            sharded,
            sharded,
            sharded,
            P("group", "head"),
            P("group", "head"),
            sharded,
            P(("group", "branch"), None),
            P(("group", "branch")),
        ),
        out_specs=(sharded, sharded, sharded, P("group", "head"), P("group", "head")),
        check_vma=False,
    )
```

```python
import functools

import jax
import jax.numpy as jnp
from jax import lax
from jax.experimental import pallas as pl
from jax.experimental.pallas import tpu as pltpu
from jax.sharding import PartitionSpec as P

QH = 32
KVH = 4
HD = 128
PER = QH // KVH
RADIX = 4
GATHER = (3, 2, 1)
SCATTER = (3, 2, 1)
SUM = (3, 2, 1)
LOG2E = 1.4426950408889634
NT = (((1,), (1,)), ((), ()))
NN = (((1,), (0,)), ((), ()))
TN = (((0,), (0,)), ((), ()))


def dot(a, b, dims):
    return lax.dot_general(a, b, dims, preferred_element_type=jnp.float32)


def digits(size):
    out, stride = [], 1
    while stride < size:
        count = min(RADIX, size // stride)
        while (size // stride) % count:
            count -= 1
        if count == 1:
            count = size // stride
        out.append((stride, count))
        stride *= count
    return out


def moved(size, stride, count, step, sign):
    pairs = []
    for i in range(size):
        digit = (i // stride) % count
        if count & (count - 1) == 0:
            other = digit ^ step
        else:
            other = (digit + sign * step) % count
        pairs.append((i, i + (other - digit) * stride))
    return pairs


def in_order(count, order):
    return [step for step in order if step < count] + list(range(len(order) + 1, count))


def exchange(blocks, axis, size, stride, steps, sign):
    count = len(steps) + 1
    return [
        lax.ppermute(block, axis, moved(size, stride, count, step, sign))
        for block, step in zip(blocks, steps)
    ]


def gather_parts(x, axis, size):
    parts = [x]
    for stride, count in digits(size):
        low = len(parts)
        block = x if low == 1 else jnp.stack(parts)
        steps = in_order(count, GATHER)
        for got in exchange([block] * (count - 1), axis, size, stride, steps, 1):
            parts += [got] if low == 1 else [got[i] for i in range(low)]
    return parts


def tree_sum(terms):
    while len(terms) > 1:
        terms = [a + b for a, b in zip(terms[::2], terms[1::2])] + terms[len(terms) & ~1 :]
    return terms[0]


def scatter_sum(parts, axis, size):
    parts = list(parts)
    for stride, count in reversed(digits(size)):
        low = len(parts) // count
        blocks = parts if low == 1 else [
            jnp.stack(parts[i * low : (i + 1) * low]) for i in range(count)
        ]
        found = dict(zip(in_order(count, GATHER), blocks[1:]))
        steps = in_order(count, SCATTER)
        terms = blocks[:1] + exchange([found[s] for s in steps], axis, size, stride, steps, -1)
        total = tree_sum([t.astype(jnp.float32) for t in terms])
        parts = [total] if low == 1 else [total[i] for i in range(low)]
    return parts[0]


def all_sum(x, axis, size):
    for stride, count in digits(size):
        steps = in_order(count, SUM)
        sent = x.astype(jnp.bfloat16)
        terms = [sent] + exchange([sent] * (count - 1), axis, size, stride, steps, 1)
        x = tree_sum([t.astype(jnp.float32) for t in terms])
    return x


def head_rows(ref, b, h):
    cols = [slice((h * PER + m) * HD, (h * PER + m + 1) * HD) for m in range(PER)]
    return jnp.concatenate([ref[b, :, c] for c in cols], axis=0)


def tree_kernel(
    q_hbm, g_hbm, bk_hbm, bv_hbm, par_ref, len_ref,
    q_ref, g_ref, bk_ref, power_ref, dweight_ref, max_ref, sum_ref, dot_ref, live_ref,
    bv_ref, sems,
):
    count, length, _ = q_ref.shape
    heads = bk_ref.shape[2] // HD
    pairs = [(q_hbm.at[0], q_ref.at[0]), (g_hbm.at[0], g_ref.at[0])]
    pairs += [(bk_hbm, bk_ref), (bv_hbm, bv_ref)]
    for b in range(1, count):
        pairs += [(q_hbm.at[b], q_ref.at[b]), (g_hbm.at[b], g_ref.at[b])]
    copies = [pltpu.make_async_copy(s, d, sems.at[i]) for i, (s, d) in enumerate(pairs)]
    for copy in copies:
        copy.start()
    slot = lax.broadcasted_iota(jnp.int32, (length, length), 0)
    token = lax.broadcasted_iota(jnp.int32, (length, length), 1)
    reaches = []
    for b in range(count):
        hit = (slot == token) | (slot == par_ref[b : b + 1, :])
        reaches.append(hit.astype(jnp.float32).astype(jnp.bfloat16))
    for rounds in range((length - 1).bit_length()):
        reaches = [jnp.minimum(dot(r, r, NN), 1.0).astype(jnp.bfloat16) for r in reaches]
    masks = [jnp.concatenate([r.astype(jnp.float32)] * PER, axis=1) > 0.5 for r in reaches]
    place = lax.broadcasted_iota(jnp.int32, (1, PER * length), 1) % length
    for b in range(count):
        for copy in copies[2 * b + 2 if b else 0 : 2 * b + 4]:
            copy.wait()
        stage = []
        for h in range(heads):
            cols = slice(h * HD, (h + 1) * HD)
            stage.append((
                dot(bk_ref[b, :, cols], head_rows(q_ref, b, h), NT),
                dot(bv_ref[b, :, cols], head_rows(g_ref, b, h), NT),
            ))
        live = (place < len_ref[:, b : b + 1]).astype(jnp.float32)
        for h, (scores, dweights) in enumerate(stage):
            i = h * count + b
            scores = jnp.where(masks[b], scores * (HD**-0.5 * LOG2E), -1e30)
            top = jnp.max(scores, axis=0, keepdims=True)
            powers = jnp.exp2(scores - top)
            power_ref[i] = powers
            dweight_ref[i] = dweights
            live_ref[i] = live
            max_ref[i] = top
            sum_ref[i] = jnp.sum(powers, axis=0, keepdims=True)
            dot_ref[i] = jnp.sum(powers * dweights, axis=0, keepdims=True)


def prefix_kernel(*refs, parts):
    q_ref, g_ref, max_ref, sum_ref, dot_ref, live_ref = refs[:6]
    pre_refs = refs[6 : 6 + parts]
    dscore_ref, scale_ref, delta_ref = refs[6 + parts : 9 + parts]
    out_refs = refs[9 + parts :]
    count, length, _ = q_ref.shape
    rows, width = pre_refs[0].shape
    width //= 2
    heads = width // HD
    factor = HD**-0.5
    pre = jnp.concatenate([r[...] for r in pre_refs], axis=0)
    lanes = lambda ref, h: jnp.concatenate([ref[h * count + b] for b in range(count)], axis=1)
    stage = []
    for h in range(heads):
        low = h * HD
        keys = pre[:, low : low + HD]
        values = pre[:, width + low : width + low + HD]
        q = jnp.concatenate([head_rows(q_ref, b, h) for b in range(count)], axis=0)
        g = jnp.concatenate([head_rows(g_ref, b, h) for b in range(count)], axis=0)
        stage.append((q, g, dot(keys, q, NT), dot(values, g, NT)))
    ready = []
    for h, (q, g, scores, dweights) in enumerate(stage):
        scores = scores * (factor * LOG2E)
        tree_max = lanes(max_ref, h)
        top = jnp.maximum(jnp.max(scores, axis=0, keepdims=True), tree_max)
        powers = jnp.exp2(scores - top)
        tree = jnp.exp2(tree_max - top)
        scale = lanes(live_ref, h) / (
            jnp.sum(powers, axis=0, keepdims=True) + tree * lanes(sum_ref, h)
        )
        delta = scale * (
            jnp.sum(powers * dweights, axis=0, keepdims=True) + tree * lanes(dot_ref, h)
        )
        weights = powers * scale
        dscores = (weights * (dweights - delta)).astype(jnp.bfloat16)
        tree_scale = scale * tree
        wide = scores.shape[1] // count
        for b in range(count):
            i, cols = h * count + b, slice(b * wide, (b + 1) * wide)
            dscore_ref[i] = dscores[:, cols]
            scale_ref[i] = tree_scale[:, cols]
            delta_ref[i] = delta[:, cols]
        ready.append((weights.astype(jnp.bfloat16), dscores))
    for h in range(heads):
        low = h * HD
        value_sum = dot(ready[h][0], stage[h][1], NN)
        key_sum = dot(ready[h][1], stage[h][0], NN) * factor
        for i, ref in enumerate(out_refs):
            ref[:, low : low + HD] = key_sum[i * rows : (i + 1) * rows].astype(ref.dtype)
            ref[:, width + low : width + low + HD] = value_sum[i * rows : (i + 1) * rows].astype(
                ref.dtype
            )


def branch_kernel(*refs, parts):
    q_ref, g_ref, bk_ref, power_ref, dweight_ref, dscore_ref, scale_ref, delta_ref = refs[:8]
    pre_refs = refs[8 : 8 + parts]
    dq_ref, dbk_ref, dbv_ref = refs[8 + parts :]
    count, length, _ = q_ref.shape
    heads = bk_ref.shape[2] // HD
    factor = HD**-0.5
    pre = jnp.concatenate([r[:, : heads * HD] for r in pre_refs], axis=0)
    ready = []
    for i in range(heads * count):
        weights = power_ref[i] * scale_ref[i]
        dscores = (weights * (dweight_ref[i] - delta_ref[i])).astype(jnp.bfloat16)
        ready.append((dscores, weights.astype(jnp.bfloat16)))
    for h in range(heads):
        low = h * HD
        for b in range(count):
            dscores, weights = ready[h * count + b]
            both = jnp.concatenate([dscore_ref[h * count + b], dscores], axis=0)
            keys = jnp.concatenate([pre[:, low : low + HD], bk_ref[b, :, low : low + HD]], axis=0)
            query_grad = (dot(both, keys, TN) * factor).astype(jnp.bfloat16)
            for m in range(PER):
                col = (h * PER + m) * HD
                dq_ref[b, :, col : col + HD] = query_grad[m * length : (m + 1) * length]
            value_grad = dot(weights, head_rows(g_ref, b, h), NN)
            key_grad = dot(dscores, head_rows(q_ref, b, h), NN) * factor
            dbk_ref[b, :, low : low + HD] = key_grad.astype(jnp.bfloat16)
            dbv_ref[b, :, low : low + HD] = value_grad.astype(jnp.bfloat16)


def body(
    queries, branch_keys, branch_values, prefix_keys, prefix_values, out_grad, parents, lengths,
    *, groups, branches
):
    count, length, columns = queries.shape
    heads = branch_keys.shape[2] // HD
    prefix = prefix_keys.shape[0] * groups
    packed = jnp.concatenate([prefix_keys, prefix_values], axis=1)
    parts = gather_parts(packed, "group", groups)
    vmem = pl.BlockSpec(memory_space=pltpu.VMEM)
    anywhere = pl.BlockSpec(memory_space=pltpu.HBM)
    hbm = lambda x: pltpu.with_memory_space_constraint(x, pltpu.HBM)
    params = pltpu.CompilerParams(vmem_limit_bytes=16 * 1024 * 1024)
    wide = PER * length
    row = jax.ShapeDtypeStruct((heads * count, 1, wide), jnp.float32)
    block = jax.ShapeDtypeStruct((heads * count, length, wide), jnp.float32)
    like = lambda x: jax.ShapeDtypeStruct(x.shape, x.dtype)
    work = heads * count * wide * HD * 2
    q, g, keys, powers, dweights, tops, sums, dots, live = pl.pallas_call(
        tree_kernel,
        out_shape=[like(queries), like(out_grad), like(branch_keys), block, block, row, row, row, row],
        in_specs=[anywhere] * 4 + [vmem] * 2,
        out_specs=[vmem] * 9,
        scratch_shapes=[
            pltpu.VMEM(branch_values.shape, branch_values.dtype),
            pltpu.SemaphoreType.DMA((2 + 2 * count,)),
        ],
        compiler_params=params,
        cost_estimate=pl.CostEstimate(
            flops=2 * work * length, bytes_accessed=2 * queries.size * 2, transcendentals=wide * length * 4
        ),
        name="tree",
    )(*(hbm(x) for x in (queries, out_grad, branch_keys, branch_values)), parents, lengths.reshape(1, count))
    outs = pl.pallas_call(
        functools.partial(prefix_kernel, parts=groups),
        out_shape=[
            jax.ShapeDtypeStruct((heads * count, prefix, wide), jnp.bfloat16), row, row
        ]
        + [jax.ShapeDtypeStruct(packed.shape, jnp.float32)]
        + [like(packed)] * (groups - 1),
        in_specs=[vmem] * (6 + groups),
        out_specs=[vmem] * (3 + groups),
        compiler_params=params,
        cost_estimate=pl.CostEstimate(
            flops=4 * work * prefix, bytes_accessed=0, transcendentals=wide * prefix * 4
        ),
        name="prefix",
    )(q, g, tops, sums, dots, live, *parts)
    query_grad, branch_key_grad, branch_value_grad = pl.pallas_call(
        functools.partial(branch_kernel, parts=groups),
        out_shape=[like(queries), like(branch_keys), like(branch_values)],
        in_specs=[vmem] * (8 + groups),
        out_specs=[vmem] * 3,
        compiler_params=params,
        cost_estimate=pl.CostEstimate(
            flops=4 * work * length, bytes_accessed=queries.size * 2, transcendentals=0
        ),
        name="branch",
    )(q, g, keys, powers, dweights, *outs[:3], *parts)
    owned = scatter_sum(outs[3:], "group", groups)
    total = all_sum(owned, "branch", branches)
    total = total.astype(jnp.bfloat16)
    half = prefix_keys.shape[1]
    return query_grad, branch_key_grad, branch_value_grad, total[:, :half], total[:, half:]


def solution(mesh):
    sharded = P(("group", "branch"), None, "head")
    return jax.shard_map(
        functools.partial(body, groups=mesh.shape["group"], branches=mesh.shape["branch"]),
        mesh=mesh,
        in_specs=(
            sharded,
            sharded,
            sharded,
            P("group", "head"),
            P("group", "head"),
            sharded,
            P(("group", "branch"), None),
            P(("group", "branch")),
        ),
        out_specs=(sharded, sharded, sharded, P("group", "head"), P("group", "head")),
        check_vma=False,
    )
```

```python
import functools

import jax
import jax.numpy as jnp
from jax import lax
from jax.experimental import pallas as pl
from jax.experimental.pallas import tpu as pltpu
from jax.sharding import PartitionSpec as P

QH = 32
KVH = 4
HD = 128
PER = QH // KVH
RADIX = 4
CYCLES = {1: (1, 3, 0, 2), 2: (3, 2, 1, 0), 3: (2, 0, 3, 1)}
GATHER = (1, 2, 3)
SCATTER = (3, 2, 1)
SUM = (3, 2, 1)
LOG2E = 1.4426950408889634
NT = (((1,), (1,)), ((), ()))
NN = (((1,), (0,)), ((), ()))
TN = (((0,), (0,)), ((), ()))


def dot(a, b, dims):
    return lax.dot_general(a, b, dims, preferred_element_type=jnp.float32)


def digits(size):
    out, stride = [], 1
    while stride < size:
        count = min(RADIX, size // stride)
        while (size // stride) % count:
            count -= 1
        if count == 1:
            count = size // stride
        out.append((stride, count))
        stride *= count
    return out


def moved(size, stride, count, step, sign):
    pairs = []
    for i in range(size):
        digit = (i // stride) % count
        if count == 4 and sign:
            cycle = CYCLES[step]
            other = cycle[digit] if sign > 0 else cycle.index(digit)
        elif count & (count - 1) == 0:
            other = digit ^ step
        else:
            other = (digit + (sign or 1) * step) % count
        pairs.append((i, i + (other - digit) * stride))
    return pairs


def in_order(count, order):
    return [step for step in order if step < count] + list(range(len(order) + 1, count))


def exchange(blocks, axis, size, stride, steps, sign):
    count = len(steps) + 1
    return [
        lax.ppermute(block, axis, moved(size, stride, count, step, sign))
        for block, step in zip(blocks, steps)
    ]


def gather_parts(x, axis, size):
    parts = [x]
    for stride, count in digits(size):
        low = len(parts)
        block = x if low == 1 else jnp.stack(parts)
        steps = in_order(count, GATHER)
        gots = exchange([block] * (count - 1), axis, size, stride, steps, 1)
        if count == 4:
            one, two, three = lax.optimization_barrier(tuple(gots))
            digit = lax.axis_index(axis) // stride % count
            outer = (digit == 0) | (digit == 3)
            gots = [two, jnp.where(outer, one, three), jnp.where(outer, three, one)]
        for got in gots:
            parts += [got] if low == 1 else [got[i] for i in range(low)]
    return parts


def tree_sum(terms):
    while len(terms) > 1:
        terms = [a + b for a, b in zip(terms[::2], terms[1::2])] + terms[len(terms) & ~1 :]
    return terms[0]


def scatter_sum(parts, axis, size):
    parts = list(parts)
    for stride, count in reversed(digits(size)):
        low = len(parts) // count
        blocks = parts if low == 1 else [
            jnp.stack(parts[i * low : (i + 1) * low]) for i in range(count)
        ]
        found = dict(zip(in_order(count, SCATTER if count == 4 else GATHER), blocks[1:]))
        steps = in_order(count, SCATTER)
        terms = blocks[:1] + exchange([found[s] for s in steps], axis, size, stride, steps, 0 if count == 4 else -1)
        total = tree_sum([t.astype(jnp.float32) for t in terms])
        parts = [total] if low == 1 else [total[i] for i in range(low)]
    return parts[0]


def all_sum(x, axis, size):
    for stride, count in digits(size):
        steps = in_order(count, SUM)
        sent = x.astype(jnp.bfloat16)
        terms = [sent] + exchange([sent] * (count - 1), axis, size, stride, steps, 0)
        x = tree_sum([t.astype(jnp.float32) for t in terms])
    return x


def head_rows(ref, b, h):
    cols = [slice((h * PER + m) * HD, (h * PER + m + 1) * HD) for m in range(PER)]
    return jnp.concatenate([ref[b, :, c] for c in cols], axis=0)


def tree_kernel(
    q_hbm, g_hbm, bk_hbm, bv_hbm, par_ref, len_ref,
    q_ref, g_ref, bk_ref, power_ref, dweight_ref, max_ref, sum_ref, dot_ref, live_ref,
    bv_ref, sems,
):
    count, length, _ = q_ref.shape
    heads = bk_ref.shape[2] // HD
    pairs = [(q_hbm.at[0], q_ref.at[0]), (g_hbm.at[0], g_ref.at[0])]
    pairs += [(bk_hbm, bk_ref), (bv_hbm, bv_ref)]
    for b in range(1, count):
        pairs += [(q_hbm.at[b], q_ref.at[b]), (g_hbm.at[b], g_ref.at[b])]
    copies = [pltpu.make_async_copy(s, d, sems.at[i]) for i, (s, d) in enumerate(pairs)]
    for copy in copies:
        copy.start()
    slot = lax.broadcasted_iota(jnp.int32, (length, length), 0)
    token = lax.broadcasted_iota(jnp.int32, (length, length), 1)
    reaches = []
    for b in range(count):
        hit = (slot == token) | (slot == par_ref[b : b + 1, :])
        reaches.append(hit.astype(jnp.float32).astype(jnp.bfloat16))
    for rounds in range((length - 1).bit_length()):
        reaches = [jnp.minimum(dot(r, r, NN), 1.0).astype(jnp.bfloat16) for r in reaches]
    masks = [jnp.concatenate([r.astype(jnp.float32)] * PER, axis=1) > 0.5 for r in reaches]
    place = lax.broadcasted_iota(jnp.int32, (1, PER * length), 1) % length
    for b in range(count):
        for copy in copies[2 * b + 2 if b else 0 : 2 * b + 4]:
            copy.wait()
        stage = []
        for h in range(heads):
            cols = slice(h * HD, (h + 1) * HD)
            stage.append((
                dot(bk_ref[b, :, cols], head_rows(q_ref, b, h), NT),
                dot(bv_ref[b, :, cols], head_rows(g_ref, b, h), NT),
            ))
        live = (place < len_ref[:, b : b + 1]).astype(jnp.float32)
        for h, (scores, dweights) in enumerate(stage):
            i = h * count + b
            scores = jnp.where(masks[b], scores * (HD**-0.5 * LOG2E), -1e30)
            top = jnp.max(scores, axis=0, keepdims=True)
            powers = jnp.exp2(scores - top)
            power_ref[i] = powers
            dweight_ref[i] = dweights
            live_ref[i] = live
            max_ref[i] = top
            sum_ref[i] = jnp.sum(powers, axis=0, keepdims=True)
            dot_ref[i] = jnp.sum(powers * dweights, axis=0, keepdims=True)


def prefix_kernel(*refs, parts):
    q_ref, g_ref, max_ref, sum_ref, dot_ref, live_ref = refs[:6]
    pre_refs = refs[6 : 6 + parts]
    dscore_ref, scale_ref, delta_ref = refs[6 + parts : 9 + parts]
    out_refs = refs[9 + parts :]
    count, length, _ = q_ref.shape
    rows, width = pre_refs[0].shape
    width //= 2
    heads = width // HD
    factor = HD**-0.5
    pre = jnp.concatenate([r[...] for r in pre_refs], axis=0)
    stage = []
    for h in range(heads):
        low = h * HD
        keys = pre[:, low : low + HD]
        values = pre[:, width + low : width + low + HD]
        for b in range(count):
            q = head_rows(q_ref, b, h)
            g = head_rows(g_ref, b, h)
            stage.append((q, g, dot(keys, q, NT), dot(values, g, NT)))
    ready = []
    for i, (q, g, scores, dweights) in enumerate(stage):
        scores = scores * (factor * LOG2E)
        tree_max = max_ref[i]
        top = jnp.maximum(jnp.max(scores, axis=0, keepdims=True), tree_max)
        powers = jnp.exp2(scores - top)
        tree = jnp.exp2(tree_max - top)
        scale = live_ref[i] / (jnp.sum(powers, axis=0, keepdims=True) + tree * sum_ref[i])
        delta = scale * (jnp.sum(powers * dweights, axis=0, keepdims=True) + tree * dot_ref[i])
        weights = powers * scale
        dscores = (weights * (dweights - delta)).astype(jnp.bfloat16)
        dscore_ref[i] = dscores
        scale_ref[i] = scale * tree
        delta_ref[i] = delta
        ready.append((weights.astype(jnp.bfloat16), dscores))
    for h in range(heads):
        low = h * HD
        key_sum = value_sum = None
        for b in range(count):
            i = h * count + b
            value_grad = dot(ready[i][0], stage[i][1], NN)
            key_grad = dot(ready[i][1], stage[i][0], NN) * factor
            key_sum = key_grad if b == 0 else key_sum + key_grad
            value_sum = value_grad if b == 0 else value_sum + value_grad
        for i, ref in enumerate(out_refs):
            ref[:, low : low + HD] = key_sum[i * rows : (i + 1) * rows].astype(ref.dtype)
            ref[:, width + low : width + low + HD] = value_sum[i * rows : (i + 1) * rows].astype(
                ref.dtype
            )


def branch_kernel(*refs, parts):
    q_ref, g_ref, bk_ref, power_ref, dweight_ref, dscore_ref, scale_ref, delta_ref = refs[:8]
    pre_refs = refs[8 : 8 + parts]
    dq_ref, dbk_ref, dbv_ref = refs[8 + parts :]
    count, length, _ = q_ref.shape
    heads = bk_ref.shape[2] // HD
    factor = HD**-0.5
    pre = jnp.concatenate([r[:, : heads * HD] for r in pre_refs], axis=0)
    for h in range(heads):
        low = h * HD
        for b in range(count):
            i = h * count + b
            weights = power_ref[i] * scale_ref[i]
            dscores = (weights * (dweight_ref[i] - delta_ref[i])).astype(jnp.bfloat16)
            tree_keys = bk_ref[b, :, low : low + HD]
            value_grad = dot(weights.astype(jnp.bfloat16), head_rows(g_ref, b, h), NN)
            key_grad = dot(dscores, head_rows(q_ref, b, h), NN) * factor
            dbk_ref[b, :, low : low + HD] = key_grad.astype(jnp.bfloat16)
            dbv_ref[b, :, low : low + HD] = value_grad.astype(jnp.bfloat16)
            both = jnp.concatenate([dscore_ref[i], dscores], axis=0)
            keys = jnp.concatenate([pre[:, low : low + HD], tree_keys], axis=0)
            query_grad = (dot(both, keys, TN) * factor).astype(jnp.bfloat16)
            for m in range(PER):
                col = (h * PER + m) * HD
                dq_ref[b, :, col : col + HD] = query_grad[m * length : (m + 1) * length]


def body(
    queries, branch_keys, branch_values, prefix_keys, prefix_values, out_grad, parents, lengths,
    *, groups, branches
):
    count, length, columns = queries.shape
    heads = branch_keys.shape[2] // HD
    prefix = prefix_keys.shape[0] * groups
    packed = jnp.concatenate([prefix_keys, prefix_values], axis=1)
    parts = gather_parts(packed, "group", groups)
    vmem = pl.BlockSpec(memory_space=pltpu.VMEM)
    anywhere = pl.BlockSpec(memory_space=pltpu.HBM)
    hbm = lambda x: pltpu.with_memory_space_constraint(x, pltpu.HBM)
    params = pltpu.CompilerParams(vmem_limit_bytes=16 * 1024 * 1024)
    wide = PER * length
    row = jax.ShapeDtypeStruct((heads * count, 1, wide), jnp.float32)
    block = jax.ShapeDtypeStruct((heads * count, length, wide), jnp.float32)
    like = lambda x: jax.ShapeDtypeStruct(x.shape, x.dtype)
    work = heads * count * wide * HD * 2
    q, g, keys, powers, dweights, tops, sums, dots, live = pl.pallas_call(
        tree_kernel,
        out_shape=[like(queries), like(out_grad), like(branch_keys), block, block, row, row, row, row],
        in_specs=[anywhere] * 4 + [vmem] * 2,
        out_specs=[vmem] * 9,
        scratch_shapes=[
            pltpu.VMEM(branch_values.shape, branch_values.dtype),
            pltpu.SemaphoreType.DMA((2 + 2 * count,)),
        ],
        compiler_params=params,
        cost_estimate=pl.CostEstimate(
            flops=2 * work * length, bytes_accessed=2 * queries.size * 2, transcendentals=wide * length * 4
        ),
        name="tree",
    )(*(hbm(x) for x in (queries, out_grad, branch_keys, branch_values)), parents, lengths.reshape(1, count))
    outs = pl.pallas_call(
        functools.partial(prefix_kernel, parts=groups),
        out_shape=[
            jax.ShapeDtypeStruct((heads * count, prefix, wide), jnp.bfloat16), row, row
        ]
        + [jax.ShapeDtypeStruct(packed.shape, jnp.float32)]
        + [like(packed)] * (groups - 1),
        in_specs=[vmem] * (6 + groups),
        out_specs=[vmem] * (3 + groups),
        compiler_params=params,
        cost_estimate=pl.CostEstimate(
            flops=4 * work * prefix, bytes_accessed=0, transcendentals=wide * prefix * 4
        ),
        name="prefix",
    )(q, g, tops, sums, dots, live, *parts)
    query_grad, branch_key_grad, branch_value_grad = pl.pallas_call(
        functools.partial(branch_kernel, parts=groups),
        out_shape=[like(queries), like(branch_keys), like(branch_values)],
        in_specs=[vmem] * (8 + groups),
        out_specs=[vmem] * 3,
        compiler_params=params,
        cost_estimate=pl.CostEstimate(
            flops=4 * work * length, bytes_accessed=queries.size * 2, transcendentals=0
        ),
        name="branch",
    )(q, g, keys, powers, dweights, *outs[:3], *parts)
    owned = scatter_sum(outs[3:], "group", groups)
    total = all_sum(owned, "branch", branches)
    total = total.astype(jnp.bfloat16)
    half = prefix_keys.shape[1]
    return query_grad, branch_key_grad, branch_value_grad, total[:, :half], total[:, half:]


def solution(mesh):
    sharded = P(("group", "branch"), None, "head")
    return jax.shard_map(
        functools.partial(body, groups=mesh.shape["group"], branches=mesh.shape["branch"]),
        mesh=mesh,
        in_specs=(
            sharded,
            sharded,
            sharded,
            P("group", "head"),
            P("group", "head"),
            sharded,
            P(("group", "branch"), None),
            P(("group", "branch")),
        ),
        out_specs=(sharded, sharded, sharded, P("group", "head"), P("group", "head")),
        check_vma=False,
    )
```
